1024 devices in a mesh: dp: 64 (over y, x), expert: 16 (over z, core).
Axes of the slice: x: 8, y: 8, z: 8, core: 2. Of those that a mesh axis runs over, the one named last changes fastest.
Arguments:
- routes: int32 [544, 4], P('expert'), may hold values from 0 to 15, all different within a row; in each aligned block of 34 rows (0 to 33, 34 to 67, ...) at most 10 rows name the same one
- probs: float32 [544, 4], P('expert'), may hold values from 0.05 to 1
- out_grad: bfloat16 [544, 6144], P('expert'), may hold values from -6 to 6
- saved_inputs: bfloat16 [16, 16, 10, 6144], P('expert'), may hold values from -6 to 6
- w_gate: bfloat16 [16, 5376, 6144], P('expert', 'dp'), may hold values from -0.078125 to 0.078125
- w_up: bfloat16 [16, 5376, 6144], P('expert', 'dp'), may hold values from -0.078125 to 0.078125
- w_down: bfloat16 [16, 5376, 6144], P('expert', 'dp'), may hold values from -0.078125 to 0.078125
Outputs:
- in_grad: bfloat16 [544, 6144], P('expert', 'dp')
- prob_grad: float32 [544, 4], P('expert')
The draws below stay inside these ranges and needn't reach their ends.
Inputs may be any that keep to these rules, and one draw needn't show every extreme that they name: `routes`: each row names 4 different experts; within one block of 34 tokens no expert is named more than 10 times, and in some block some expert is named exactly 10 times.
All inputs are finite; a program needn't handle non-finite values.
Results may differ from the reference program's by a relative error of at most 0.012.
Values may be sent and summed in bfloat16 or wider, within the bound.
No kernel may reach another device: no remote copies, remote signals or barrier semaphores. Data moves between devices by JAX's collectives and lax.ppermute only.
A program may use at most 128 MiB of HBM per device.

```python
import math
import jax
import jax.numpy as jnp
import numpy as np
from jax import lax

D = 6144
TOP = 4
TOK_DEV = 34
EXPERTS = 16
FF = 5376
CAP = 10
TOKENS = 544


def block_levels(rng, dims, pieces, smallest, high):
    level = 1.0
    for dim, shards_of in pieces:
        heights = jax.random.uniform(jax.random.fold_in(jax.random.fold_in(rng, 6), dim), (shards_of,), jnp.float32, smallest / len(pieces), high / len(pieces))
        level = level * jnp.repeat(jnp.exp(heights), dims[dim] // shards_of).reshape((-1,) + (1,) * (len(dims) - 1 - dim))
    return level


def routed_block(rng, own, number, rows, amount, top, reach, slope):
    order = jax.random.permutation(rng, amount)
    crowded, ordinary = shares(amount, rows * top, reach, slope, True), shares(amount, rows * top, reach, slope, False)
    places = jnp.arange(amount)

    def named(sizes, turn):
        used = int((sizes > 0).sum())
        fixed = max(1, used // 4)
        passed = fixed + (places - fixed + turn * (used - fixed)) % max(1, amount - fixed)
        return jnp.zeros((amount,), jnp.int32).at[order[jnp.where(places < fixed, places, passed)]].set(jnp.asarray(sizes, jnp.int32))

    sizes = jnp.where(number % 4 == 0, named(crowded, number // 4), named(ordinary, number - number // 4 - 1))
    mixed = jax.random.permutation(jax.random.fold_in(own, 3), amount)
    donor, sink = mixed[0:amount // 2 * 2:2], mixed[1:amount // 2 * 2:2]
    room = jnp.minimum(sizes[donor] - 1, reach - sizes[sink]) // 2
    room = jnp.where((donor == order[0]) | (sink == order[0]) | (sizes[sink] == 0), 0, jnp.maximum(room, 0))
    passed = jax.random.randint(jax.random.fold_in(own, 4), (amount // 2,), 0, 1 << 20) % (room + 1)
    sizes = sizes.at[donor].add(-passed).at[sink].add(passed)
    labels = jnp.searchsorted(jnp.cumsum(sizes), jnp.arange(rows * top), side="right").astype(jnp.int32)
    grid = labels.reshape(top, rows).T
    grid = grid[jax.random.permutation(jax.random.fold_in(own, 1), rows)]
    turn = jax.random.randint(jax.random.fold_in(own, 2), (rows, 1), 0, top)
    return jnp.take_along_axis(grid, (jnp.arange(top)[None, :] + turn) % top, axis=1)


def shares(count, total, most, slope, full):
    weights = [(1 << 20) // math.isqrt(standing ** slope) + 1 for standing in range(1, count + 1)]
    largest = most if full else min(most, max(-(-total // count), total * weights[0] // sum(weights)))
    least = 1 if total - largest >= count - 1 else 0
    holding, spare = [largest] + [least] * (count - 1), total - largest - least * (count - 1)
    while spare > 0:
        candidates = [i for i in range(1, count) if holding[i] < largest] or [i for i in range(1, count) if holding[i] < most]
        pool, remaining = sum([weights[i] for i in candidates]), spare
        for i in candidates:
            more = min(most - holding[i], max(1, remaining * weights[i] // pool), spare)
            holding[i] = holding[i] + more
            spare = spare - more
    return np.array(holding)


def scatter_about(key, extent, width, most, shards=(), held_as=jnp.bfloat16):
    result = jax.random.normal(key, extent, jnp.float32) * width
    if len(shards) > 0:
        result = block_levels(key, extent, shards, -0.22, 0.18) * result
    return jnp.clip(result, min=-most, max=most).astype(held_as)


def setup_inputs(seed: int = 0) -> dict:
    seeds = jax.random.split(jax.random.key(seed), 8)
    routes_keys = jax.random.split(jax.random.fold_in(seeds[0], 1), TOKENS // TOK_DEV)
    routes_turns = jax.random.permutation(jax.random.fold_in(seeds[0], 3), TOKENS // TOK_DEV)
    routes = jax.vmap(lambda own, number: routed_block(jax.random.fold_in(seeds[0], 2), own, number, TOK_DEV, EXPERTS, TOP, CAP, 1))(routes_keys, routes_turns).reshape((TOKENS, TOP))
    probs = jnp.clip(jnp.exp(math.log(1.0) - 2.9957323 * jax.random.uniform(seeds[1], (TOKENS, TOP), jnp.float32) ** block_levels(seeds[1], (TOKENS, TOP), ((0, 16),), -0.2, 0.2)), 0.05, 1.0)
    out_grad = scatter_about(seeds[2], (TOKENS, D), 1.0, 6.0, ((0, 16),))
    saved_inputs = scatter_about(seeds[3], (EXPERTS, EXPERTS, CAP, D), 1.0, 6.0, ((0, 16),))
    w_gate = scatter_about(seeds[4], (EXPERTS, FF, D), D ** -0.5, 0.078125, ((0, 16), (1, 64)))
    w_up = scatter_about(seeds[5], (EXPERTS, FF, D), D ** -0.5, 0.078125, ((0, 16), (1, 64)))
    w_down = scatter_about(seeds[6], (EXPERTS, FF, D), FF ** -0.5, 0.078125, ((0, 16), (1, 64)))
    return dict(routes=routes, probs=probs, out_grad=out_grad, saved_inputs=saved_inputs, w_gate=w_gate, w_up=w_up, w_down=w_down)


def route_slots(blocks):
    one_hot = (blocks[..., None] == jnp.arange(EXPERTS, dtype=jnp.int32)[None, None, :]).astype(jnp.int32)
    before = jnp.cumsum(one_hot, axis=1) - one_hot
    position = jnp.sum(before * one_hot, axis=2).astype(jnp.int32)
    return (blocks * CAP + position).astype(jnp.int32)


def dispatch(slots, values, weights):
    grads = jnp.zeros((EXPERTS * CAP, D), jnp.bfloat16).at[slots].set(values)
    scales = jnp.zeros((EXPERTS * CAP,), jnp.bfloat16).at[slots].set(weights)
    return grads, scales


def one_expert(operands):
    inputs, gate_weight, up_weight, down_weight, grads, scales = operands
    inputs = inputs.reshape(EXPERTS * CAP, D)
    grads = grads.reshape(EXPERTS * CAP, D)
    scales = scales.reshape(EXPERTS * CAP)
    contract = (((1,), (1,)), ((), ()))
    gate_pre = lax.dot_general(inputs, gate_weight, contract, preferred_element_type=jnp.float32)
    up_pre = lax.dot_general(inputs, up_weight, contract, preferred_element_type=jnp.float32)
    sigmoid_gate = jax.nn.sigmoid(gate_pre)
    silu_gate = gate_pre * sigmoid_gate
    hidden = (silu_gate * up_pre).astype(jnp.bfloat16)
    back = lax.dot_general(grads, down_weight, contract, preferred_element_type=jnp.float32)
    prob_sum = jnp.sum(hidden.astype(jnp.float32) * back, axis=1)
    scaled = scales.astype(jnp.float32)[:, None] * back
    d_gate = (scaled * up_pre * sigmoid_gate * (1.0 + gate_pre * (1.0 - sigmoid_gate))).astype(jnp.bfloat16)
    d_up = (scaled * silu_gate).astype(jnp.bfloat16)
    slot_grads = jnp.dot(d_gate, gate_weight, preferred_element_type=jnp.float32)
    slot_grads = slot_grads + jnp.dot(d_up, up_weight, preferred_element_type=jnp.float32)
    return slot_grads.astype(jnp.bfloat16), prob_sum.astype(jnp.bfloat16)


def collect(slots, grads, prob_values):
    picked = grads[slots].astype(jnp.float32).reshape(TOK_DEV, TOP, D)
    return jnp.sum(picked, axis=1).astype(jnp.bfloat16), prob_values[slots].astype(jnp.float32)


def reference(routes, probs, out_grad, saved_inputs, w_gate, w_up, w_down):
    blocks = routes.reshape(EXPERTS, TOK_DEV * TOP).astype(jnp.int32)
    slot_index = route_slots(blocks)
    token_rows = out_grad.reshape(EXPERTS, TOK_DEV, D)
    route_rows = jnp.repeat(token_rows, TOP, axis=1)
    route_probs = probs.reshape(EXPERTS, TOK_DEV * TOP).astype(jnp.bfloat16)
    grad_slots, prob_slots = jax.vmap(dispatch)(slot_index, route_rows, route_probs)
    grad_slots = grad_slots.reshape(EXPERTS, EXPERTS, CAP, D).transpose(1, 0, 2, 3)
    prob_slots = prob_slots.reshape(EXPERTS, EXPERTS, CAP).transpose(1, 0, 2)
    slot_grads, prob_back = lax.map(one_expert, (saved_inputs, w_gate, w_up, w_down, grad_slots, prob_slots))
    slot_grads = slot_grads.reshape(EXPERTS, EXPERTS, CAP, D).transpose(1, 0, 2, 3).reshape(EXPERTS, EXPERTS * CAP, D)
    prob_back = prob_back.reshape(EXPERTS, EXPERTS, CAP).transpose(1, 0, 2).reshape(EXPERTS, EXPERTS * CAP)
    in_grad, prob_grad = jax.vmap(collect)(slot_index, slot_grads, prob_back)
    return in_grad.reshape(TOKENS, D), prob_grad.reshape(TOKENS, TOP)
```

```python
import jax
import jax.numpy as jnp
from jax import lax
from jax.experimental import pallas as pl
from jax.experimental.pallas import tpu as pltpu
from jax.sharding import Mesh
from jax.sharding import PartitionSpec as P

F32 = jnp.float32
BF16 = jnp.bfloat16
LANES = 128
PAD = 16
SIDE = 8
VMEM_LIMIT = 48 * 1024 * 1024
HELD = jnp.bfloat16


def iota(shape, dim):
    return lax.broadcasted_iota(jnp.int32, shape, dim)


def one_hot(mask):
    return jnp.where(mask, 1.0, 0.0).astype(BF16)


def dot(a, b):
    return jnp.dot(a, b, preferred_element_type=F32)


def params(**more):
    return pltpu.CompilerParams(vmem_limit_bytes=VMEM_LIMIT, **more)


def vmem():
    return pl.BlockSpec(memory_space=pltpu.VMEM)


def pick_kernel(capacity, place, routes, probs, grad_x, grad_y, send, picker):
    rows, tokens = picker.shape
    row = iota((rows, tokens), 0)
    expert, slot = row // PAD, row % PAD
    named = jnp.zeros((rows, tokens), F32)
    weight = jnp.zeros((rows, tokens), F32)
    for k in range(routes.shape[0]):
        hit = routes[k : k + 1, :] == expert
        named = named + jnp.where(hit, 1.0, 0.0)
        weight = weight + jnp.where(hit, probs[k : k + 1, :], 0.0)
    earlier = one_hot(iota((tokens, tokens), 0) < iota((tokens, tokens), 1))
    before = dot(named.astype(BF16), earlier)
    chosen = (named > 0.0) & (before == slot.astype(F32)) & (slot < capacity)
    hot = one_hot(chosen)
    picker[...] = hot
    scale = jnp.sum(jnp.where(chosen, weight, 0.0), axis=1, keepdims=True)
    spread = jnp.where(iota((rows, LANES), 1) == iota((rows, LANES), 0) % PAD, scale, 0.0)
    to_row, from_row = iota((rows, rows), 0), iota((rows, rows), 1)
    gather = one_hot((to_row // PAD == from_row // PAD) & (to_row % PAD == capacity))
    weight_rows = dot(gather, spread.astype(BF16))
    part = grad_x.shape[1]
    even = (iota((rows, part), 0) // PAD) % 2 == 0
    picked = jnp.where(even, dot(hot, grad_x[...]), dot(hot, grad_y[...]))
    send[:, :LANES] = (picked[:, :LANES] + weight_rows).astype(BF16)
    send[:, LANES:] = picked[:, LANES:].astype(BF16)


def pick(place, routes, probs, out_grad, capacity, experts):
    tokens, width = out_grad.shape
    part = width // SIDE
    choices = routes.shape[0]
    rows = experts * PAD
    whole = lambda shape: pl.BlockSpec(shape, lambda i, at: (0, 0))

    def body(*refs):
        pick_kernel(capacity, *refs)

    return pl.pallas_call(
        body,
        grid_spec=pltpu.PrefetchScalarGridSpec(
            num_scalar_prefetch=1,
            grid=(1,),
            in_specs=[
                whole((choices, tokens)),
                whole((choices, tokens)),
                pl.BlockSpec((tokens, part), lambda i, at: (0, at[0])),
                pl.BlockSpec((tokens, part), lambda i, at: (0, at[1])),
            ],
            out_specs=[whole((rows, part)), whole((rows, tokens))],
        ),
        out_shape=[
            jax.ShapeDtypeStruct((rows, part), BF16),
            jax.ShapeDtypeStruct((rows, tokens), BF16),
        ],
        compiler_params=params(),
        name="pick",
    )(place, routes, probs, out_grad, out_grad)


def spread_kernel(capacity, recv, out, scale):
    rows, experts = recv.shape[0], recv.shape[0] // PAD
    slots = experts * capacity
    to_row, from_row = iota((slots, rows), 0), iota((slots, rows), 1)
    first = (to_row % experts) * PAD
    order = one_hot(from_row == first + to_row // experts)
    moved = dot(order, recv[...]).astype(BF16)
    for peer in range(out.shape[0]):
        out[peer] = moved
    weights = dot(one_hot(from_row == first + capacity), recv[:, :LANES])
    own = iota((slots, LANES), 1) == iota((slots, LANES), 0) // experts
    column = jnp.sum(jnp.where(own, weights, 0.0), axis=1, keepdims=True)
    scale[...] = jnp.broadcast_to(column, scale.shape)


def spread(recv, capacity):
    rows, width = recv.shape
    slots = rows // PAD * capacity
    shards = jax.ShapeDtypeStruct((SIDE, slots, width), BF16)

    def body(*refs):
        spread_kernel(capacity, *refs)

    return pl.pallas_call(
        body,
        in_specs=[vmem()],
        out_specs=[vmem()] * 2,
        out_shape=[shards, jax.ShapeDtypeStruct((slots, LANES), F32)],
        compiler_params=params(),
        name="spread",
    )(recv)


def forward_kernel(inputs, w_gate, w_up, gate_pre, up_pre):
    contract = (((1,), (1,)), ((), ()))

    @pl.when(pl.program_id(0) == 0)
    def _():
        gate_pre[...] = jnp.zeros_like(gate_pre)
        up_pre[...] = jnp.zeros_like(up_pre)

    x = inputs[...]
    gate_pre[...] += lax.dot_general(x, w_gate[...], contract, preferred_element_type=F32)
    up_pre[...] += lax.dot_general(x, w_up[...], contract, preferred_element_type=F32)


def forward(inputs, w_gate, w_up):
    slots, width = inputs.shape
    hidden = w_gate.shape[0]
    steps = 4
    piece = lambda rows: pl.BlockSpec((rows, width // steps), lambda i: (0, i))
    whole = pl.BlockSpec((slots, hidden), lambda i: (0, 0))
    shape = jax.ShapeDtypeStruct((slots, hidden), F32)
    return pl.pallas_call(
        forward_kernel,
        grid=(steps,),
        in_specs=[piece(slots), piece(hidden), piece(hidden)],
        out_specs=[whole, whole],
        out_shape=[shape, shape],
        compiler_params=params(),
        cost_estimate=pl.CostEstimate(
            flops=4 * slots * hidden * width,
            bytes_accessed=2 * width * (slots + 2 * hidden),
            transcendentals=0,
        ),
        name="forward",
    )(inputs, w_gate, w_up)


def pack_sums(total):
    high = total.astype(BF16).astype(F32)
    return jnp.where(iota(total.shape, 1) < LANES // 2, high, total - high).astype(BF16)


def unpack_sums(packed):
    return packed + pltpu.roll(packed, LANES // 2, axis=1)


def cut(source, first, width, lane):
    done = 0
    while done < width:
        src, dst = first + done, lane + done
        take = min(width - done, LANES - src % LANES, LANES - dst % LANES)
        shift = (dst - src) % LANES
        values = source(src // LANES)
        if shift:
            values = pltpu.roll(values, shift, axis=1)
        yield dst // LANES, dst % LANES, dst % LANES + take, values
        done += take


def slot_grads_kernel(
    capacity, core, grads, w_down, gate_pre, up_pre, scale, w_gate, w_up, out, held
):
    contract = (((1,), (1,)), ((), ()))
    peers, slots, part = grads.shape
    hidden = w_down.shape[0]
    back = jnp.zeros((slots, hidden), F32)
    for peer in range(peers):
        columns = slice(peer * part, (peer + 1) * part)
        back = back + lax.dot_general(
            grads[peer], w_down[:, columns], contract, preferred_element_type=F32
        )
    gate, up = gate_pre[...], up_pre[...]
    sigmoid_gate = jax.nn.sigmoid(gate)
    silu_gate = gate * sigmoid_gate
    activated = (silu_gate * up).astype(BF16).astype(F32)
    sums = jnp.sum(activated * back, axis=1, keepdims=True)
    scaled = scale[:, :1] * back
    d_gate = (scaled * up * sigmoid_gate * (1.0 + gate * (1.0 - sigmoid_gate))).astype(BF16)
    d_up = (scaled * silu_gate).astype(BF16)

    experts = slots // capacity
    grid = jnp.where(iota((slots, LANES), 1) % (LANES // 2) == iota((slots, LANES), 0) % experts, sums, 0.0)
    rows = [jnp.sum(grid[c * experts : (c + 1) * experts], axis=0, keepdims=True) for c in range(capacity)]
    total = jnp.zeros((PAD, LANES), F32)
    for c, line in enumerate(rows):
        total = jnp.where(iota((PAD, LANES), 0) == c, line, total)
    packed = pack_sums(total)

    block = w_gate.shape[1] // SIDE
    tiles = block // LANES
    share = block // SIDE
    for y in range(SIDE):
        columns = slice(y * block, (y + 1) * block)
        grad = dot(d_gate, w_gate[:, columns]) + dot(d_up, w_up[:, columns])
        held[:, columns] = grad.astype(held.dtype)
    for peer in range(SIDE):
        out[peer, tiles * slots :, :] = packed

    def tile_of(tile):
        return held[:, tile * LANES : (tile + 1) * LANES]

    @pl.when(core[0] == 0)
    def _():
        lane = iota((slots, LANES), 1)
        for x in range(SIDE):
            made = [None] * tiles
            for y in range(SIDE):
                for tile, low, high, values in cut(tile_of, y * block + x * share, share, y * share):
                    if made[tile] is None:
                        made[tile] = values
                    else:
                        made[tile] = jnp.where((lane >= low) & (lane < high), values, made[tile])
            for j in range(tiles):
                out[x, j * slots : (j + 1) * slots, :] = made[j].astype(BF16)

    @pl.when(core[0] == 1)
    def _():
        for y in range(SIDE):
            for j in range(tiles):
                out[y, j * slots : (j + 1) * slots, :] = tile_of(y * tiles + j).astype(BF16)


def slot_grads(core, grads, w_down, gate_pre, up_pre, scale, w_gate, w_up, capacity):
    slots = scale.shape[0]
    width = w_gate.shape[1]
    rows = width // SIDE // LANES * slots + PAD

    def body(*refs):
        slot_grads_kernel(capacity, *refs)

    return pl.pallas_call(
        body,
        in_specs=[pl.BlockSpec(memory_space=pltpu.SMEM)] + [vmem()] * 7,
        out_specs=vmem(),
        out_shape=jax.ShapeDtypeStruct((SIDE, rows, LANES), BF16),
        scratch_shapes=[pltpu.VMEM((slots, width), HELD)],
        compiler_params=params(),
        name="slot_grads",
    )(core, grads, w_down, gate_pre, up_pre, scale, w_gate, w_up)


def total(recv, first, count):
    sums = recv[0, first : first + count].astype(F32)
    for peer in range(1, recv.shape[0]):
        sums = sums + recv[peer, first : first + count].astype(F32)
    return sums


def first_sum_kernel(recv, out):
    peers, rows, _ = recv.shape
    slots = out.shape[1] - PAD
    tiles = (rows - PAD) // slots
    share = tiles * LANES // peers
    columns = [total(recv, j * slots, slots) for j in range(tiles)]
    packed = pack_sums(unpack_sums(total(recv, tiles * slots, PAD)))
    lane = iota((slots, LANES), 1)
    for peer in range(peers):
        made = None
        for _, low, high, values in cut(lambda tile: columns[tile], peer * share, share, 0):
            made = values if made is None else jnp.where((lane >= low) & (lane < high), values, made)
        out[peer, :slots, :] = made.astype(BF16)
        out[peer, slots:, :] = packed


def first_sum(recv, slots):
    return pl.pallas_call(
        first_sum_kernel,
        in_specs=[vmem()],
        out_specs=vmem(),
        out_shape=jax.ShapeDtypeStruct((SIDE, slots + PAD, LANES), BF16),
        compiler_params=params(),
        name="first_sum",
    )(recv)


def second_sum_kernel(share, recv, out):
    slots, rows = recv.shape[1] - PAD, out.shape[0]
    experts = rows // PAD
    grads = total(recv, 0, slots)
    probs = unpack_sums(total(recv, slots, PAD)).astype(BF16)
    line = dot(one_hot(iota((slots, PAD), 0) // experts == iota((slots, PAD), 1)), probs)
    lane, row = iota((slots, LANES), 1), iota((slots, LANES), 0)
    column = jnp.sum(jnp.where(lane == row % experts, line, 0.0), axis=1, keepdims=True)
    values = jnp.where(lane < share, grads, jnp.where(lane == share, column, 0.0)).astype(BF16)
    to_row, from_row = iota((rows, slots), 0), iota((rows, slots), 1)
    order = one_hot(from_row == (to_row % PAD) * experts + to_row // PAD)
    out[...] = dot(order, values).astype(BF16)


def second_sum(recv, share, experts):
    def body(*refs):
        second_sum_kernel(share, *refs)

    return pl.pallas_call(
        body,
        in_specs=[vmem()],
        out_specs=vmem(),
        out_shape=jax.ShapeDtypeStruct((experts * PAD, LANES), BF16),
        compiler_params=params(),
        name="second_sum",
    )(recv)


def combine_kernel(routes, picker, recv, in_grad, prob_grad):
    share = in_grad.shape[1]
    hot, values = picker[...], recv[...]
    summed = lax.dot_general(hot, values, (((0,), (0,)), ((), ())), preferred_element_type=F32)
    in_grad[...] = summed[:, :share].astype(BF16)
    column = values[:, share : share + 1].astype(F32)
    found = jnp.where(hot.astype(F32) > 0.0, column, 0.0)
    expert = iota(hot.shape, 0) // PAD
    for k in range(routes.shape[0]):
        hit = routes[k : k + 1, :] == expert
        prob_grad[k : k + 1, :] = jnp.sum(jnp.where(hit, found, 0.0), axis=0, keepdims=True)


def combine(routes, picker, recv, share):
    choices, tokens = routes.shape
    return pl.pallas_call(
        combine_kernel,
        in_specs=[vmem()] * 3,
        out_specs=[vmem()] * 2,
        out_shape=[
            jax.ShapeDtypeStruct((tokens, share), BF16),
            jax.ShapeDtypeStruct((choices, tokens), F32),
        ],
        compiler_params=params(),
        name="combine",
    )(routes, picker, recv)


def exchange(values):
    return lax.all_to_all(values, "expert", split_axis=0, concat_axis=0, tiled=True)


def exchange_in_plane(values, even_along_x):
    experts = lax.axis_size("expert")
    groups = []
    for expert in range(experts):
        along_x = (expert % 2 == 0) == even_along_x
        for line in range(SIDE):
            group = [(line, i) if along_x else (i, line) for i in range(SIDE)]
            groups.append([(y * SIDE + x) * experts + expert for y, x in group])
    return lax.all_to_all(
        values, ("y", "x", "expert"), split_axis=0, concat_axis=0, axis_index_groups=groups, tiled=True
    )


def on_device(routes, probs, out_grad, saved_inputs, w_gate, w_up, w_down):
    experts = lax.axis_size("expert")
    capacity = saved_inputs.shape[2]
    width = out_grad.shape[1]
    share = width // (SIDE * SIDE)
    slots = experts * capacity
    routes = routes.T
    rounded = probs.T.astype(BF16).astype(F32)
    place = jnp.stack([lax.axis_index("x"), lax.axis_index("y")]).astype(jnp.int32)
    core = (lax.axis_index("expert") % 2).astype(jnp.int32).reshape(1)

    send, picker = pick(place, routes, rounded, out_grad, capacity, experts)
    recv = exchange(send.reshape(experts, PAD, -1)).reshape(experts * PAD, -1)
    inputs = saved_inputs[0].transpose(1, 0, 2).reshape(slots, width)
    gate_pre, up_pre = forward(inputs, w_gate[0], w_up[0])

    shards, scale = spread(recv, capacity)
    grads = exchange_in_plane(shards, True)
    parts = slot_grads(
        core, grads, w_down[0], gate_pre, up_pre, scale, w_gate[0], w_up[0], capacity
    )
    first = first_sum(exchange_in_plane(parts, True), slots)
    back = second_sum(exchange_in_plane(first, False), share, experts)
    got = exchange(back.reshape(experts, PAD, LANES)).reshape(experts * PAD, LANES)
    in_grad, prob_grad = combine(routes, picker, got, share)
    return in_grad, prob_grad.T


def solution(mesh):
    grid = Mesh(mesh.devices.reshape(SIDE, SIDE, -1), ("y", "x", "expert"))
    dp = ("y", "x")
    placed = (
        P("expert", None),
        P("expert", None),
        P("expert", None),
        P("expert", None, None, None),
        P("expert", dp, None),
        P("expert", dp, None),
        P("expert", dp, None),
    )
    return jax.shard_map(
        on_device,
        mesh=grid,
        in_specs=placed,
        out_specs=(P("expert", dp), P("expert", None)),
        check_vma=False,
    )
```

```python
import jax
import jax.numpy as jnp
from jax import lax
from jax.experimental import pallas as pl
from jax.experimental.pallas import tpu as pltpu
from jax.sharding import Mesh
from jax.sharding import PartitionSpec as P

F32 = jnp.float32
BF16 = jnp.bfloat16
LANES = 128
PAD = 16
SIDE = 8
MIB = 1024 * 1024
HELD = jnp.bfloat16


def iota(shape, dim):
    return lax.broadcasted_iota(jnp.int32, shape, dim)


def one_hot(mask):
    return jnp.where(mask, 1.0, 0.0).astype(BF16)


def dot(a, b):
    return jnp.dot(a, b, preferred_element_type=F32)


def swap(values):
    row, source = iota((PAD * PAD, PAD * PAD), 0), iota((PAD * PAD, PAD * PAD), 1)
    order = one_hot(source == (row % PAD) * PAD + row // PAD)
    return dot(order, values).astype(values.dtype)


def params(mib):
    return pltpu.CompilerParams(vmem_limit_bytes=mib * MIB)


def vmem():
    return pl.BlockSpec(memory_space=pltpu.VMEM)


def hbm():
    return pl.BlockSpec(memory_space=pltpu.HBM)


def smem():
    return pl.BlockSpec(memory_space=pltpu.SMEM)


def pick_kernel(
    capacity, place, routes_in, probs_in, out_grad, send, picker, routes, probs, grad_x, grad_y, sems
):
    slots, tokens = picker.shape
    experts = slots // capacity
    tiles = grad_x.shape[1] // LANES
    copies = [
        pltpu.make_async_copy(routes_in, routes, sems.at[0]),
        pltpu.make_async_copy(probs_in, probs, sems.at[1]),
    ]
    for axis, grad in enumerate((grad_x, grad_y)):
        width = grad.shape[1]
        first = pl.multiple_of(place[axis] * width, LANES)
        copies.append(
            pltpu.make_async_copy(out_grad.at[:, pl.ds(first, width)], grad, sems.at[2 + axis])
        )
    for copy in copies:
        copy.start()
    copies[0].wait()
    copies[1].wait()
    row = iota((slots, tokens), 0)
    expert, slot = row % experts, row // experts
    named = jnp.zeros((slots, tokens), F32)
    weight = jnp.zeros((slots, tokens), F32)
    rounded = probs[...].astype(BF16).astype(F32)
    for k in range(routes.shape[0]):
        hit = routes[k : k + 1, :] == expert
        named = named + jnp.where(hit, 1.0, 0.0)
        weight = weight + jnp.where(hit, rounded[k : k + 1, :], 0.0)
    earlier = one_hot(iota((tokens, tokens), 0) < iota((tokens, tokens), 1))
    before = dot(named.astype(BF16), earlier)
    chosen = (named > 0.0) & (before == slot.astype(F32))
    hot = one_hot(chosen)
    picker[...] = hot
    scale = jnp.sum(jnp.where(chosen, weight, 0.0), axis=1, keepdims=True)
    lane = iota((experts, LANES), 1)
    weights = jnp.zeros((experts, LANES), F32)
    for c in range(capacity):
        weights = jnp.where(lane == c, scale[c * experts : (c + 1) * experts], weights)
    copies[2].wait()
    copies[3].wait()
    even = iota((slots, LANES), 0) % 2 == 0
    pieces = []
    for j in range(tiles):
        columns = slice(j * LANES, (j + 1) * LANES)
        picked = jnp.where(even, dot(hot, grad_x[:, columns]), dot(hot, grad_y[:, columns]))
        pieces.append(picked.astype(BF16))
    chunk = send.shape[0] // experts
    spare = chunk - tiles * capacity - 1
    pieces += [weights.astype(BF16), jnp.zeros((spare * experts, LANES), BF16)]
    rows = jnp.concatenate(pieces, axis=0)
    for g in range(chunk // PAD):
        group = swap(rows[g * PAD * PAD : (g + 1) * PAD * PAD])
        for e in range(experts):
            send[e * chunk + g * PAD : e * chunk + (g + 1) * PAD, :] = group[e * PAD : (e + 1) * PAD]


def pick(place, routes, probs, out_grad, capacity, experts):
    tokens, width = out_grad.shape
    part = width // SIDE
    choices = routes.shape[0]
    chunk = -(-(part // LANES * capacity + 1) // PAD) * PAD

    def body(*refs):
        pick_kernel(capacity, *refs)

    return pl.pallas_call(
        body,
        in_specs=[smem(), hbm(), hbm(), hbm()],
        out_specs=[vmem()] * 2,
        out_shape=[
            jax.ShapeDtypeStruct((experts * chunk, LANES), BF16),
            jax.ShapeDtypeStruct((experts * capacity, tokens), BF16),
        ],
        scratch_shapes=[
            pltpu.VMEM((choices, tokens), jnp.int32),
            pltpu.VMEM((choices, tokens), F32),
            pltpu.VMEM((tokens, part), BF16),
            pltpu.VMEM((tokens, part), BF16),
            pltpu.SemaphoreType.DMA((4,)),
        ],
        compiler_params=params(63),
        name="pick",
    )(place, routes, probs, out_grad)


def spread_kernel(capacity, recv, out, scale, held, sems):
    chunk = recv.shape[0] // PAD
    moved = []
    for g in range(chunk // PAD):
        group = [recv[s * chunk + g * PAD : s * chunk + (g + 1) * PAD, :] for s in range(PAD)]
        moved.append(swap(jnp.concatenate(group, axis=0)))
    rows = jnp.concatenate(moved, axis=0)
    kept = held.shape[0]
    held[...] = rows[:kept]
    copies = [pltpu.make_async_copy(held, out.at[i], sems.at[i]) for i in range(out.shape[0])]
    for copy in copies:
        copy.start()
    weights = rows[kept : kept + PAD].astype(F32)
    for c in range(capacity):
        column = jnp.broadcast_to(weights[:, c : c + 1], (PAD, LANES))
        scale[c * PAD : (c + 1) * PAD, :] = column
    for copy in copies:
        copy.wait()


def spread(recv, part, capacity):
    slots = PAD * capacity
    kept = part // LANES * slots

    def body(*refs):
        spread_kernel(capacity, *refs)

    return pl.pallas_call(
        body,
        in_specs=[vmem()],
        out_specs=[hbm(), vmem()],
        out_shape=[
            jax.ShapeDtypeStruct((SIDE, kept, LANES), BF16),
            jax.ShapeDtypeStruct((slots, LANES), F32),
        ],
        scratch_shapes=[pltpu.VMEM((kept, LANES), BF16), pltpu.SemaphoreType.DMA((SIDE,))],
        compiler_params=params(58),
        name="spread",
    )(recv)


def forward_kernel(inputs, w_gate, w_up, gate_pre, up_pre):
    contract = (((1,), (1,)), ((), ()))

    @pl.when(pl.program_id(0) == 0)
    def _():
        gate_pre[...] = jnp.zeros_like(gate_pre)
        up_pre[...] = jnp.zeros_like(up_pre)

    x = inputs[...]
    gate_pre[...] += lax.dot_general(x, w_gate[...], contract, preferred_element_type=F32)
    up_pre[...] += lax.dot_general(x, w_up[...], contract, preferred_element_type=F32)


def forward(inputs, w_gate, w_up):
    slots, width = inputs.shape
    hidden = w_gate.shape[0]
    steps = 4
    piece = lambda rows: pl.BlockSpec((rows, width // steps), lambda i: (0, i))
    whole = pl.BlockSpec((slots, hidden), lambda i: (0, 0))
    shape = jax.ShapeDtypeStruct((slots, hidden), F32)
    return pl.pallas_call(
        forward_kernel,
        grid=(steps,),
        in_specs=[piece(slots), piece(hidden), piece(hidden)],
        out_specs=[whole, whole],
        out_shape=[shape, shape],
        compiler_params=params(32),
        cost_estimate=pl.CostEstimate(
            flops=4 * slots * hidden * width,
            bytes_accessed=2 * width * (slots + 2 * hidden),
            transcendentals=0,
        ),
        name="forward",
    )(inputs, w_gate, w_up)


def pack_sums(total):
    high = total.astype(BF16).astype(F32)
    return jnp.where(iota(total.shape, 1) < LANES // 2, high, total - high).astype(BF16)


def unpack_sums(packed):
    return packed + pltpu.roll(packed, LANES // 2, axis=1)


def cut(source, first, width, lane):
    done = 0
    while done < width:
        src, dst = first + done, lane + done
        take = min(width - done, LANES - src % LANES, LANES - dst % LANES)
        shift = (dst - src) % LANES
        values = source(src // LANES)
        if shift:
            values = pltpu.roll(values, shift, axis=1)
        yield dst // LANES, dst % LANES, dst % LANES + take, values
        done += take


def slot_grads_kernel(
    capacity, core, grads, down_in, gate_pre, up_pre, scale, gate_in, up_in, out, held, w_down, w_gate, w_up, sems
):
    loads = [
        pltpu.make_async_copy(source, target, sems.at[i])
        for i, (source, target) in enumerate(((down_in, w_down), (gate_in, w_gate), (up_in, w_up)))
    ]
    for load in loads:
        load.start()
    contract = (((1,), (1,)), ((), ()))
    peers, slots, hidden = grads.shape[0], scale.shape[0], w_down.shape[0]
    part = w_down.shape[1] // peers
    back = jnp.zeros((slots, hidden), F32)
    loads[0].wait()
    for peer in range(peers):
        columns = slice(peer * part, (peer + 1) * part)
        tiles = [grads[peer, j * slots : (j + 1) * slots, :] for j in range(part // LANES)]
        back = back + lax.dot_general(
            jnp.concatenate(tiles, axis=1), w_down[:, columns], contract, preferred_element_type=F32
        )
    gate, up = gate_pre[...], up_pre[...]
    sigmoid_gate = jax.nn.sigmoid(gate)
    silu_gate = gate * sigmoid_gate
    activated = (silu_gate * up).astype(BF16).astype(F32)
    sums = jnp.sum(activated * back, axis=1, keepdims=True)
    scaled = scale[:, :1] * back
    d_gate = (scaled * up * sigmoid_gate * (1.0 + gate * (1.0 - sigmoid_gate))).astype(BF16)
    d_up = (scaled * silu_gate).astype(BF16)

    experts = slots // capacity
    grid = jnp.where(iota((slots, LANES), 1) % (LANES // 2) == iota((slots, LANES), 0) % experts, sums, 0.0)
    rows = [jnp.sum(grid[c * experts : (c + 1) * experts], axis=0, keepdims=True) for c in range(capacity)]
    total = jnp.zeros((PAD, LANES), F32)
    for c, line in enumerate(rows):
        total = jnp.where(iota((PAD, LANES), 0) == c, line, total)
    packed = pack_sums(total)

    block = w_gate.shape[1] // SIDE
    tiles = block // LANES
    share = block // SIDE
    loads[1].wait()
    loads[2].wait()
    for y in range(SIDE):
        columns = slice(y * block, (y + 1) * block)
        grad = dot(d_gate, w_gate[:, columns]) + dot(d_up, w_up[:, columns])
        held[:, columns] = grad.astype(held.dtype)
    for peer in range(SIDE):
        out[peer, tiles * slots :, :] = packed

    def tile_of(tile):
        return held[:, tile * LANES : (tile + 1) * LANES]

    @pl.when(core[0] == 0)
    def _():
        lane = iota((slots, LANES), 1)
        for x in range(SIDE):
            made = [None] * tiles
            for y in range(SIDE):
                for tile, low, high, values in cut(tile_of, y * block + x * share, share, y * share):
                    if made[tile] is None:
                        made[tile] = values
                    else:
                        made[tile] = jnp.where((lane >= low) & (lane < high), values, made[tile])
            for j in range(tiles):
                out[x, j * slots : (j + 1) * slots, :] = made[j].astype(BF16)

    @pl.when(core[0] == 1)
    def _():
        for y in range(SIDE):
            for j in range(tiles):
                out[y, j * slots : (j + 1) * slots, :] = tile_of(y * tiles + j).astype(BF16)


def slot_grads(core, grads, w_down, gate_pre, up_pre, scale, w_gate, w_up, capacity):
    slots = scale.shape[0]
    width = w_gate.shape[1]
    rows = width // SIDE // LANES * slots + PAD

    def body(*refs):
        slot_grads_kernel(capacity, *refs)

    return pl.pallas_call(
        body,
        in_specs=[smem(), vmem(), hbm()] + [vmem()] * 3 + [hbm()] * 2,
        out_specs=vmem(),
        out_shape=jax.ShapeDtypeStruct((SIDE, rows, LANES), BF16),
        scratch_shapes=[
            pltpu.VMEM((slots, width), HELD),
            *[pltpu.VMEM(w_down.shape, BF16)] * 3,
            pltpu.SemaphoreType.DMA((3,)),
        ],
        compiler_params=params(58),
        name="slot_grads",
    )(core, grads, w_down, gate_pre, up_pre, scale, w_gate, w_up)


def total(recv, first, count):
    sums = recv[0, first : first + count].astype(F32)
    for peer in range(1, recv.shape[0]):
        sums = sums + recv[peer, first : first + count].astype(F32)
    return sums


def first_sum_kernel(recv, out):
    peers, rows, _ = recv.shape
    slots = out.shape[1] - PAD
    tiles = (rows - PAD) // slots
    share = tiles * LANES // peers
    columns = [total(recv, j * slots, slots) for j in range(tiles)]
    packed = pack_sums(unpack_sums(total(recv, tiles * slots, PAD)))
    lane = iota((slots, LANES), 1)
    for peer in range(peers):
        made = None
        for _, low, high, values in cut(lambda tile: columns[tile], peer * share, share, 0):
            made = values if made is None else jnp.where((lane >= low) & (lane < high), values, made)
        out[peer, :slots, :] = made.astype(BF16)
        out[peer, slots:, :] = packed


def first_sum(recv, slots):
    return pl.pallas_call(
        first_sum_kernel,
        in_specs=[vmem()],
        out_specs=vmem(),
        out_shape=jax.ShapeDtypeStruct((SIDE, slots + PAD, LANES), BF16),
        compiler_params=params(32),
        name="first_sum",
    )(recv)


def second_sum_kernel(share, recv, out):
    slots, rows = recv.shape[1] - PAD, out.shape[0]
    experts = rows // PAD
    grads = total(recv, 0, slots)
    probs = unpack_sums(total(recv, slots, PAD)).astype(BF16)
    line = dot(one_hot(iota((slots, PAD), 0) // experts == iota((slots, PAD), 1)), probs)
    lane, row = iota((slots, LANES), 1), iota((slots, LANES), 0)
    column = jnp.sum(jnp.where(lane == row % experts, line, 0.0), axis=1, keepdims=True)
    values = jnp.where(lane < share, grads, jnp.where(lane == share, column, 0.0)).astype(BF16)
    out[...] = swap(jnp.concatenate([values, jnp.zeros((rows - slots, LANES), BF16)], axis=0))


def second_sum(recv, share, experts):
    def body(*refs):
        second_sum_kernel(share, *refs)

    return pl.pallas_call(
        body,
        in_specs=[vmem()],
        out_specs=vmem(),
        out_shape=jax.ShapeDtypeStruct((experts * PAD, LANES), BF16),
        compiler_params=params(32),
        name="second_sum",
    )(recv)


def combine_kernel(routes, picker, recv, in_grad, prob_grad):
    share = in_grad.shape[1]
    hot = picker[...]
    values = swap(recv[...])[: hot.shape[0]]
    summed = lax.dot_general(hot, values, (((0,), (0,)), ((), ())), preferred_element_type=F32)
    in_grad[...] = summed[:, :share].astype(BF16)
    column = values[:, share : share + 1].astype(F32)
    found = jnp.where(hot.astype(F32) > 0.0, column, 0.0)
    expert = iota(hot.shape, 0) % PAD
    for k in range(routes.shape[0]):
        hit = routes[k : k + 1, :] == expert
        prob_grad[k : k + 1, :] = jnp.sum(jnp.where(hit, found, 0.0), axis=0, keepdims=True)


def combine(routes, picker, recv, share):
    choices, tokens = routes.shape
    return pl.pallas_call(
        combine_kernel,
        in_specs=[vmem()] * 3,
        out_specs=[vmem()] * 2,
        out_shape=[
            jax.ShapeDtypeStruct((tokens, share), BF16),
            jax.ShapeDtypeStruct((choices, tokens), F32),
        ],
        compiler_params=params(32),
        name="combine",
    )(routes, picker, recv)


def exchange(values):
    return lax.all_to_all(values, "expert", split_axis=0, concat_axis=0, tiled=True)


def exchange_in_plane(values, even_along_x):
    experts = lax.axis_size("expert")
    groups = []
    for expert in range(experts):
        along_x = (expert % 2 == 0) == even_along_x
        for line in range(SIDE):
            group = [(line, i) if along_x else (i, line) for i in range(SIDE)]
            groups.append([(y * SIDE + x) * experts + expert for y, x in group])
    return lax.all_to_all(
        values, ("y", "x", "expert"), split_axis=0, concat_axis=0, axis_index_groups=groups, tiled=True
    )


def on_device(routes, probs, out_grad, saved_inputs, w_gate, w_up, w_down):
    experts = lax.axis_size("expert")
    capacity = saved_inputs.shape[2]
    width = out_grad.shape[1]
    share = width // (SIDE * SIDE)
    slots = experts * capacity
    routes = routes.T
    probs = probs.T
    place = jnp.stack([lax.axis_index("x"), lax.axis_index("y")]).astype(jnp.int32)
    core = (lax.axis_index("expert") & 1).astype(jnp.int32).reshape(1)

    send, picker = pick(place, routes, probs, out_grad, capacity, experts)
    recv = exchange(send.reshape(experts, -1, LANES)).reshape(-1, LANES)
    inputs = saved_inputs[0].transpose(1, 0, 2).reshape(slots, width)
    gate_pre, up_pre = forward(inputs, w_gate[0], w_up[0])

    shards, scale = spread(recv, width // SIDE, capacity)
    grads = exchange_in_plane(shards, True)
    parts = slot_grads(
        core, grads, w_down[0], gate_pre, up_pre, scale, w_gate[0], w_up[0], capacity
    )
    first = first_sum(exchange_in_plane(parts, True), slots)
    back = second_sum(exchange_in_plane(first, False), share, experts)
    got = exchange(back.reshape(experts, PAD, LANES)).reshape(experts * PAD, LANES)
    in_grad, prob_grad = combine(routes, picker, got, share)
    return in_grad, prob_grad.T


def solution(mesh):
    grid = Mesh(mesh.devices.reshape(SIDE, SIDE, -1), ("y", "x", "expert"))
    dp = ("y", "x")
    placed = (
        P("expert", None),
        P("expert", None),
        P("expert", None),
        P("expert", None, None, None),
        P("expert", dp, None),
        P("expert", dp, None),
        P("expert", dp, None),
    )
    return jax.shard_map(
        on_device,
        mesh=grid,
        in_specs=placed,
        out_specs=(P("expert", dp), P("expert", None)),
        check_vma=False,
    )
```

```python
import jax
import jax.numpy as jnp
from jax import lax
from jax.experimental import pallas as pl
from jax.experimental.pallas import tpu as pltpu
from jax.sharding import Mesh
from jax.sharding import PartitionSpec as P

F32 = jnp.float32
BF16 = jnp.bfloat16
LANES = 128
PAD = 16
SIDE = 8
MIB = 1024 * 1024
HELD = jnp.bfloat16


def iota(shape, dim):
    return lax.broadcasted_iota(jnp.int32, shape, dim)


def one_hot(mask):
    return jnp.where(mask, 1.0, 0.0).astype(BF16)


def dot(a, b):
    return jnp.dot(a, b, preferred_element_type=F32)


def swap(values):
    row, source = iota((PAD * PAD, PAD * PAD), 0), iota((PAD * PAD, PAD * PAD), 1)
    order = one_hot(source == (row % PAD) * PAD + row // PAD)
    return dot(order, values).astype(values.dtype)


def params(mib):
    return pltpu.CompilerParams(vmem_limit_bytes=mib * MIB)


def vmem():
    return pl.BlockSpec(memory_space=pltpu.VMEM)


def hbm():
    return pl.BlockSpec(memory_space=pltpu.HBM)


def smem():
    return pl.BlockSpec(memory_space=pltpu.SMEM)


def pick_kernel(
    capacity, at_x, at_y, routes_in, probs_in, out_grad, send, picker, routes, probs, grad_x, grad_y, sems
):
    slots, tokens = picker.shape
    experts = slots // capacity
    tiles = grad_x.shape[1] // LANES
    copies = [
        pltpu.make_async_copy(routes_in, routes, sems.at[0]),
        pltpu.make_async_copy(probs_in, probs, sems.at[1]),
    ]
    for axis, (at, grad) in enumerate(((at_x, grad_x), (at_y, grad_y))):
        width = grad.shape[1]
        first = pl.multiple_of(at[0] * width, LANES)
        copies.append(
            pltpu.make_async_copy(out_grad.at[:, pl.ds(first, width)], grad, sems.at[2 + axis])
        )
    for copy in copies:
        copy.start()
    copies[0].wait()
    copies[1].wait()
    row = iota((slots, tokens), 0)
    expert, slot = row % experts, row // experts
    named = jnp.zeros((slots, tokens), F32)
    weight = jnp.zeros((slots, tokens), F32)
    rounded = probs[...].astype(BF16).astype(F32)
    for k in range(routes.shape[0]):
        hit = routes[k : k + 1, :] == expert
        named = named + jnp.where(hit, 1.0, 0.0)
        weight = weight + jnp.where(hit, rounded[k : k + 1, :], 0.0)
    earlier = one_hot(iota((tokens, tokens), 0) < iota((tokens, tokens), 1))
    before = dot(named.astype(BF16), earlier)
    chosen = (named > 0.0) & (before == slot.astype(F32))
    hot = one_hot(chosen)
    picker[...] = hot
    scale = jnp.sum(jnp.where(chosen, weight, 0.0), axis=1, keepdims=True)
    lane = iota((experts, LANES), 1)
    weights = jnp.zeros((experts, LANES), F32)
    for c in range(capacity):
        weights = jnp.where(lane == c, scale[c * experts : (c + 1) * experts], weights)
    copies[2].wait()
    copies[3].wait()
    even = iota((slots, LANES), 0) % 2 == 0
    pieces = []
    for j in range(tiles):
        columns = slice(j * LANES, (j + 1) * LANES)
        picked = jnp.where(even, dot(hot, grad_x[:, columns]), dot(hot, grad_y[:, columns]))
        pieces.append(picked.astype(BF16))
    chunk = send.shape[0] // experts
    spare = chunk - tiles * capacity - 1
    pieces += [weights.astype(BF16), jnp.zeros((spare * experts, LANES), BF16)]
    rows = jnp.concatenate(pieces, axis=0)
    for g in range(chunk // PAD):
        group = swap(rows[g * PAD * PAD : (g + 1) * PAD * PAD])
        for e in range(experts):
            send[e * chunk + g * PAD : e * chunk + (g + 1) * PAD, :] = group[e * PAD : (e + 1) * PAD]


def pick(at_x, at_y, routes, probs, out_grad, capacity, experts):
    tokens, width = out_grad.shape
    part = width // SIDE
    choices = routes.shape[0]
    chunk = -(-(part // LANES * capacity + 1) // PAD) * PAD

    def body(*refs):
        pick_kernel(capacity, *refs)

    return pl.pallas_call(
        body,
        in_specs=[smem(), smem(), hbm(), hbm(), hbm()],
        out_specs=[vmem()] * 2,
        out_shape=[
            jax.ShapeDtypeStruct((experts * chunk, LANES), BF16),
            jax.ShapeDtypeStruct((experts * capacity, tokens), BF16),
        ],
        scratch_shapes=[
            pltpu.VMEM((choices, tokens), jnp.int32),
            pltpu.VMEM((choices, tokens), F32),
            pltpu.VMEM((tokens, part), BF16),
            pltpu.VMEM((tokens, part), BF16),
            pltpu.SemaphoreType.DMA((4,)),
        ],
        compiler_params=params(63),
        name="pick",
    )(at_x, at_y, routes, probs, out_grad)


def spread_kernel(capacity, recv, after, out, scale):
    chunk = recv.shape[0] // PAD
    moved = []
    for g in range(chunk // PAD):
        group = [recv[s * chunk + g * PAD : s * chunk + (g + 1) * PAD, :] for s in range(PAD)]
        moved.append(swap(jnp.concatenate(group, axis=0)))
    rows = jnp.concatenate(moved, axis=0)
    kept = out.shape[1]
    for peer in range(out.shape[0]):
        out[peer] = rows[:kept]
    weights = rows[kept : kept + PAD].astype(F32)
    for c in range(capacity):
        column = jnp.broadcast_to(weights[:, c : c + 1], (PAD, LANES))
        scale[c * PAD : (c + 1) * PAD, :] = column


def spread(recv, after, part, capacity):
    slots = PAD * capacity
    kept = part // LANES * slots

    def body(*refs):
        spread_kernel(capacity, *refs)

    return pl.pallas_call(
        body,
        in_specs=[vmem(), hbm()],
        out_specs=[vmem(), vmem()],
        out_shape=[
            jax.ShapeDtypeStruct((SIDE, kept, LANES), BF16),
            jax.ShapeDtypeStruct((slots, LANES), F32),
        ],
        compiler_params=params(32),
        name="spread",
    )(recv, after)


def forward_kernel(inputs, gate_in, up_in, down_in, both, down, activated, by_gate, by_up, pre):
    contract = (((1,), (1,)), ((), ()))
    hidden, pad = gate_in.shape[0], down.shape[0]
    step = pl.program_id(0)
    zeros = jnp.zeros((pad - hidden, gate_in.shape[1]), BF16)
    weights = jnp.concatenate([gate_in[...], zeros, up_in[...], zeros], axis=0)
    both[...] = weights
    down[...] = jnp.concatenate([down_in[...], zeros], axis=0)
    part = lax.dot_general(inputs[...], weights, contract, preferred_element_type=F32)

    @pl.when(step == 0)
    def _():
        pre[...] = part

    @pl.when(step > 0)
    def _():
        pre[...] += part

    @pl.when(step == pl.num_programs(0) - 1)
    def _():
        gate, up = pre[:, :pad], pre[:, pad:]
        sigmoid_gate = jax.nn.sigmoid(gate)
        silu_gate = gate * sigmoid_gate
        activated[...] = (silu_gate * up).astype(BF16).astype(F32)
        by_gate[...] = up * sigmoid_gate * (1.0 + gate * (1.0 - sigmoid_gate))
        by_up[...] = silu_gate


def forward(inputs, w_gate, w_up, w_down):
    slots, width = inputs.shape
    hidden = w_gate.shape[0]
    pad = -(-hidden // 32) * 32
    steps = 4
    piece = lambda rows: pl.BlockSpec((rows, width // steps), lambda i: (0, i))
    factors = pl.BlockSpec((slots, pad), lambda i: (0, 0))
    shape = jax.ShapeDtypeStruct((slots, pad), F32)
    return pl.pallas_call(
        forward_kernel,
        grid=(steps,),
        in_specs=[piece(slots), piece(hidden), piece(hidden), piece(hidden)],
        out_specs=[piece(2 * pad), piece(pad), factors, factors, factors],
        out_shape=[
            jax.ShapeDtypeStruct((2 * pad, width), BF16),
            jax.ShapeDtypeStruct((pad, width), BF16),
            shape,
            shape,
            shape,
        ],
        scratch_shapes=[pltpu.VMEM((slots, 2 * pad), F32)],
        compiler_params=params(32),
        cost_estimate=pl.CostEstimate(
            flops=4 * slots * hidden * width,
            bytes_accessed=4 * width * (slots + 3 * hidden),
            transcendentals=0,
        ),
        name="forward",
    )(inputs, w_gate, w_up, w_down)


def pack_sums(total):
    high = total.astype(BF16).astype(F32)
    return jnp.where(iota(total.shape, 1) < LANES // 2, high, total - high).astype(BF16)


def unpack_sums(packed):
    return packed + pltpu.roll(packed, LANES // 2, axis=1)


def cut(source, first, width, lane):
    done = 0
    while done < width:
        src, dst = first + done, lane + done
        take = min(width - done, LANES - src % LANES, LANES - dst % LANES)
        shift = (dst - src) % LANES
        values = source(src // LANES)
        if shift:
            values = pltpu.roll(values, shift, axis=1)
        yield dst // LANES, dst % LANES, dst % LANES + take, values
        done += take


def slot_grads_kernel(
    capacity, expert, grads, down, activated, by_gate, by_up, scale, both, out, held
):
    contract = (((1,), (1,)), ((), ()))
    peers, slots, pad = grads.shape[0], scale.shape[0], down.shape[0]
    part = down.shape[1] // peers
    back = jnp.zeros((slots, pad), F32)
    for peer in range(peers):
        columns = slice(peer * part, (peer + 1) * part)
        tiles = [grads[peer, j * slots : (j + 1) * slots, :] for j in range(part // LANES)]
        back = back + lax.dot_general(
            jnp.concatenate(tiles, axis=1), down[:, columns], contract, preferred_element_type=F32
        )
    sums = jnp.sum(activated[...] * back, axis=1, keepdims=True)
    scaled = scale[:, :1] * back
    d_gate, d_up = (scaled * by_gate[...]).astype(BF16), (scaled * by_up[...]).astype(BF16)
    d_both = jnp.concatenate([d_gate, d_up], axis=1)

    experts = slots // capacity
    grid = jnp.where(iota((slots, LANES), 1) % (LANES // 2) == iota((slots, LANES), 0) % experts, sums, 0.0)
    rows = [jnp.sum(grid[c * experts : (c + 1) * experts], axis=0, keepdims=True) for c in range(capacity)]
    total = jnp.zeros((PAD, LANES), F32)
    for c, line in enumerate(rows):
        total = jnp.where(iota((PAD, LANES), 0) == c, line, total)
    packed = pack_sums(total)

    block = both.shape[1] // SIDE
    tiles = block // LANES
    share = block // SIDE
    for y in range(SIDE):
        columns = slice(y * block, (y + 1) * block)
        held[:, columns] = dot(d_both, both[:, columns]).astype(held.dtype)
    for peer in range(SIDE):
        out[peer, tiles * slots :, :] = packed

    def tile_of(tile):
        return held[:, tile * LANES : (tile + 1) * LANES]

    @pl.when(expert[0] % 2 == 0)
    def _():
        lane = iota((slots, LANES), 1)
        for x in range(SIDE):
            made = [None] * tiles
            for y in range(SIDE):
                for tile, low, high, values in cut(tile_of, y * block + x * share, share, y * share):
                    if made[tile] is None:
                        made[tile] = values
                    else:
                        made[tile] = jnp.where((lane >= low) & (lane < high), values, made[tile])
            for j in range(tiles):
                out[x, j * slots : (j + 1) * slots, :] = made[j].astype(BF16)

    @pl.when(expert[0] % 2 == 1)
    def _():
        for y in range(SIDE):
            for j in range(tiles):
                out[y, j * slots : (j + 1) * slots, :] = tile_of(y * tiles + j).astype(BF16)


def slot_grads(expert, grads, down, activated, by_gate, by_up, scale, both, capacity):
    slots = scale.shape[0]
    width = both.shape[1]
    rows = width // SIDE // LANES * slots + PAD

    def body(*refs):
        slot_grads_kernel(capacity, *refs)

    return pl.pallas_call(
        body,
        in_specs=[smem()] + [vmem()] * 7,
        out_specs=vmem(),
        out_shape=jax.ShapeDtypeStruct((SIDE, rows, LANES), BF16),
        scratch_shapes=[pltpu.VMEM((slots, width), HELD)],
        compiler_params=params(32),
        name="slot_grads",
    )(expert, grads, down, activated, by_gate, by_up, scale, both)


def total(recv, first, count):
    sums = recv[0, first : first + count].astype(F32)
    for peer in range(1, recv.shape[0]):
        sums = sums + recv[peer, first : first + count].astype(F32)
    return sums


def first_sum_kernel(recv, out):
    peers, rows, _ = recv.shape
    slots = out.shape[1] - PAD
    tiles = (rows - PAD) // slots
    share = tiles * LANES // peers
    columns = [total(recv, j * slots, slots) for j in range(tiles)]
    packed = pack_sums(unpack_sums(total(recv, tiles * slots, PAD)))
    lane = iota((slots, LANES), 1)
    for peer in range(peers):
        made = None
        for _, low, high, values in cut(lambda tile: columns[tile], peer * share, share, 0):
            made = values if made is None else jnp.where((lane >= low) & (lane < high), values, made)
        out[peer, :slots, :] = made.astype(BF16)
        out[peer, slots:, :] = packed


def first_sum(recv, slots):
    return pl.pallas_call(
        first_sum_kernel,
        in_specs=[vmem()],
        out_specs=vmem(),
        out_shape=jax.ShapeDtypeStruct((SIDE, slots + PAD, LANES), BF16),
        compiler_params=params(32),
        name="first_sum",
    )(recv)


def second_sum_kernel(share, recv, out):
    slots, rows = recv.shape[1] - PAD, out.shape[0]
    experts = rows // PAD
    grads = total(recv, 0, slots)
    probs = unpack_sums(total(recv, slots, PAD)).astype(BF16)
    line = dot(one_hot(iota((slots, PAD), 0) // experts == iota((slots, PAD), 1)), probs)
    lane, row = iota((slots, LANES), 1), iota((slots, LANES), 0)
    column = jnp.sum(jnp.where(lane == row % experts, line, 0.0), axis=1, keepdims=True)
    values = jnp.where(lane < share, grads, jnp.where(lane == share, column, 0.0)).astype(BF16)
    out[...] = swap(jnp.concatenate([values, jnp.zeros((rows - slots, LANES), BF16)], axis=0))


def second_sum(recv, share, experts):
    def body(*refs):
        second_sum_kernel(share, *refs)

    return pl.pallas_call(
        body,
        in_specs=[vmem()],
        out_specs=vmem(),
        out_shape=jax.ShapeDtypeStruct((experts * PAD, LANES), BF16),
        compiler_params=params(32),
        name="second_sum",
    )(recv)


def combine_kernel(routes, picker, recv, in_grad, prob_grad):
    share = in_grad.shape[1]
    hot = picker[...]
    values = swap(recv[...])[: hot.shape[0]]
    summed = lax.dot_general(hot, values, (((0,), (0,)), ((), ())), preferred_element_type=F32)
    in_grad[...] = summed[:, :share].astype(BF16)
    column = values[:, share : share + 1].astype(F32)
    found = jnp.where(hot.astype(F32) > 0.0, column, 0.0)
    expert = iota(hot.shape, 0) % PAD
    for k in range(routes.shape[0]):
        hit = routes[k : k + 1, :] == expert
        prob_grad[k : k + 1, :] = jnp.sum(jnp.where(hit, found, 0.0), axis=0, keepdims=True)


def combine(routes, picker, recv, share):
    choices, tokens = routes.shape
    return pl.pallas_call(
        combine_kernel,
        in_specs=[vmem()] * 3,
        out_specs=[vmem()] * 2,
        out_shape=[
            jax.ShapeDtypeStruct((tokens, share), BF16),
            jax.ShapeDtypeStruct((choices, tokens), F32),
        ],
        compiler_params=params(32),
        name="combine",
    )(routes, picker, recv)


def exchange(values):
    return lax.all_to_all(values, "expert", split_axis=0, concat_axis=0, tiled=True)


def exchange_in_plane(values, even_along_x):
    experts = lax.axis_size("expert")
    groups = []
    for expert in range(experts):
        along_x = (expert % 2 == 0) == even_along_x
        for line in range(SIDE):
            group = [(line, i) if along_x else (i, line) for i in range(SIDE)]
            groups.append([(y * SIDE + x) * experts + expert for y, x in group])
    return lax.all_to_all(
        values, ("y", "x", "expert"), split_axis=0, concat_axis=0, axis_index_groups=groups, tiled=True
    )


def on_device(routes, probs, out_grad, saved_inputs, w_gate, w_up, w_down):
    experts = lax.axis_size("expert")
    capacity = saved_inputs.shape[2]
    width = out_grad.shape[1]
    share = width // (SIDE * SIDE)
    slots = experts * capacity
    routes = routes.T
    probs = probs.T
    at_x, at_y, expert = (
        lax.axis_index(axis).astype(jnp.int32).reshape(1) for axis in ("x", "y", "expert")
    )

    send, picker = pick(at_x, at_y, routes, probs, out_grad, capacity, experts)
    recv = exchange(send.reshape(experts, -1, LANES)).reshape(-1, LANES)
    inputs = saved_inputs[0].transpose(1, 0, 2).reshape(slots, width)
    both, down, activated, by_gate, by_up = forward(inputs, w_gate[0], w_up[0], w_down[0])

    shards, scale = spread(recv, activated, width // SIDE, capacity)
    grads = exchange_in_plane(shards, True)
    parts = slot_grads(expert, grads, down, activated, by_gate, by_up, scale, both, capacity)
    first = first_sum(exchange_in_plane(parts, True), slots)
    back = second_sum(exchange_in_plane(first, False), share, experts)
    got = exchange(back.reshape(experts, PAD, LANES)).reshape(experts * PAD, LANES)
    in_grad, prob_grad = combine(routes, picker, got, share)
    return in_grad, prob_grad.T


def solution(mesh):
    grid = Mesh(mesh.devices.reshape(SIDE, SIDE, -1), ("y", "x", "expert"))
    dp = ("y", "x")
    placed = (
        P("expert", None),
        P("expert", None),
        P("expert", None),
        P("expert", None, None, None),
        P("expert", dp, None),
        P("expert", dp, None),
        P("expert", dp, None),
    )
    return jax.shard_map(
        on_device,
        mesh=grid,
        in_specs=placed,
        out_specs=(P("expert", dp), P("expert", None)),
        check_vma=False,
    )
```

```python
import jax
import jax.numpy as jnp
from jax import lax
from jax.experimental import pallas as pl
from jax.experimental.pallas import tpu as pltpu
from jax.sharding import Mesh
from jax.sharding import PartitionSpec as P

F32 = jnp.float32
BF16 = jnp.bfloat16
LANES = 128
PAD = 16
SIDE = 8
MIB = 1024 * 1024
HELD = jnp.bfloat16


def iota(shape, dim):
    return lax.broadcasted_iota(jnp.int32, shape, dim)


def one_hot(mask):
    return jnp.where(mask, 1.0, 0.0).astype(BF16)


def dot(a, b):
    return jnp.dot(a, b, preferred_element_type=F32)


def swap(values):
    row, source = iota((PAD * PAD, PAD * PAD), 0), iota((PAD * PAD, PAD * PAD), 1)
    order = one_hot(source == (row % PAD) * PAD + row // PAD)
    return dot(order, values).astype(values.dtype)


def params(mib):
    return pltpu.CompilerParams(vmem_limit_bytes=mib * MIB)


def vmem():
    return pl.BlockSpec(memory_space=pltpu.VMEM)


def hbm():
    return pl.BlockSpec(memory_space=pltpu.HBM)


def smem():
    return pl.BlockSpec(memory_space=pltpu.SMEM)


def pick_kernel(
    capacity, at_x, at_y, _, routes_in, probs_in, out_grad, send, picker, routes, probs, grad_x, grad_y, sems
):
    slots, tokens = picker.shape
    experts = slots // capacity
    tiles = grad_x.shape[1] // LANES
    copies = [
        pltpu.make_async_copy(routes_in, routes, sems.at[0]),
        pltpu.make_async_copy(probs_in, probs, sems.at[1]),
    ]
    for axis, (at, grad) in enumerate(((at_x, grad_x), (at_y, grad_y))):
        width = grad.shape[1]
        first = pl.multiple_of(at[0] * width, LANES)
        copies.append(
            pltpu.make_async_copy(out_grad.at[:, pl.ds(first, width)], grad, sems.at[2 + axis])
        )
    for copy in copies:
        copy.start()
    copies[0].wait()
    copies[1].wait()
    row = iota((slots, tokens), 0)
    expert, slot = row % experts, row // experts
    named = jnp.zeros((slots, tokens), F32)
    weight = jnp.zeros((slots, tokens), F32)
    rounded = probs[...].astype(BF16).astype(F32)
    for k in range(routes.shape[0]):
        hit = routes[k : k + 1, :] == expert
        named = named + jnp.where(hit, 1.0, 0.0)
        weight = weight + jnp.where(hit, rounded[k : k + 1, :], 0.0)
    earlier = one_hot(iota((tokens, tokens), 0) < iota((tokens, tokens), 1))
    before = dot(named.astype(BF16), earlier)
    chosen = (named > 0.0) & (before == slot.astype(F32))
    hot = one_hot(chosen)
    picker[...] = hot
    scale = jnp.sum(jnp.where(chosen, weight, 0.0), axis=1, keepdims=True)
    lane = iota((experts, LANES), 1)
    weights = jnp.zeros((experts, LANES), F32)
    for c in range(capacity):
        weights = jnp.where(lane == c, scale[c * experts : (c + 1) * experts], weights)
    copies[2].wait()
    copies[3].wait()
    even = iota((slots, LANES), 0) % 2 == 0
    pieces = []
    for j in range(tiles):
        columns = slice(j * LANES, (j + 1) * LANES)
        picked = jnp.where(even, dot(hot, grad_x[:, columns]), dot(hot, grad_y[:, columns]))
        pieces.append(picked.astype(BF16))
    chunk = send.shape[0] // experts
    spare = chunk - tiles * capacity - 1
    pieces += [weights.astype(BF16), jnp.zeros((spare * experts, LANES), BF16)]
    rows = jnp.concatenate(pieces, axis=0)
    for g in range(chunk // PAD):
        group = swap(rows[g * PAD * PAD : (g + 1) * PAD * PAD])
        for e in range(experts):
            send[e * chunk + g * PAD : e * chunk + (g + 1) * PAD, :] = group[e * PAD : (e + 1) * PAD]


def pick(at_x, at_y, expert, routes, probs, out_grad, capacity, experts):
    tokens, width = out_grad.shape
    part = width // SIDE
    choices = routes.shape[0]
    chunk = -(-(part // LANES * capacity + 1) // PAD) * PAD

    def body(*refs):
        pick_kernel(capacity, *refs)

    return pl.pallas_call(
        body,
        in_specs=[smem(), smem(), smem(), hbm(), hbm(), hbm()],
        out_specs=[vmem()] * 2,
        out_shape=[
            jax.ShapeDtypeStruct((experts * chunk, LANES), BF16),
            jax.ShapeDtypeStruct((experts * capacity, tokens), BF16),
        ],
        scratch_shapes=[
            pltpu.VMEM((choices, tokens), jnp.int32),
            pltpu.VMEM((choices, tokens), F32),
            pltpu.VMEM((tokens, part), BF16),
            pltpu.VMEM((tokens, part), BF16),
            pltpu.SemaphoreType.DMA((4,)),
        ],
        compiler_params=params(63),
        name="pick",
    )(at_x, at_y, expert, routes, probs, out_grad)


def spread_kernel(capacity, recv, after, out, scale):
    chunk = recv.shape[0] // PAD
    moved = []
    for g in range(chunk // PAD):
        group = [recv[s * chunk + g * PAD : s * chunk + (g + 1) * PAD, :] for s in range(PAD)]
        moved.append(swap(jnp.concatenate(group, axis=0)))
    rows = jnp.concatenate(moved, axis=0)
    kept = out.shape[1]
    for peer in range(out.shape[0]):
        out[peer] = rows[:kept]
    weights = rows[kept : kept + PAD].astype(F32)
    for c in range(capacity):
        column = jnp.broadcast_to(weights[:, c : c + 1], (PAD, LANES))
        scale[c * PAD : (c + 1) * PAD, :] = column


def spread(recv, after, part, capacity):
    slots = PAD * capacity
    kept = part // LANES * slots

    def body(*refs):
        spread_kernel(capacity, *refs)

    return pl.pallas_call(
        body,
        in_specs=[vmem(), pl.BlockSpec(memory_space=pl.ANY)],
        out_specs=[vmem(), vmem()],
        out_shape=[
            jax.ShapeDtypeStruct((SIDE, kept, LANES), BF16),
            jax.ShapeDtypeStruct((slots, LANES), F32),
        ],
        compiler_params=params(32),
        name="spread",
    )(recv, after)


def forward_kernel(inputs, gate_in, up_in, down_in, both, down, factors, pre):
    contract = (((1,), (1,)), ((), ()))
    hidden, pad = gate_in.shape[0], down.shape[0]
    step = pl.program_id(0)
    zeros = jnp.zeros((pad - hidden, gate_in.shape[1]), BF16)
    weights = jnp.concatenate([gate_in[...], zeros, up_in[...], zeros], axis=0)
    both[...] = weights
    down[...] = jnp.concatenate([down_in[...], zeros], axis=0)
    part = lax.dot_general(inputs[...], weights, contract, preferred_element_type=F32)

    @pl.when(step == 0)
    def _():
        pre[...] = part

    @pl.when(step > 0)
    def _():
        pre[...] += part

    @pl.when(step == pl.num_programs(0) - 1)
    def _():
        gate, up = pre[:, :pad], pre[:, pad:]
        sigmoid_gate = jax.nn.sigmoid(gate)
        silu_gate = gate * sigmoid_gate
        factors[0] = (silu_gate * up).astype(BF16).astype(F32)
        factors[1] = up * sigmoid_gate * (1.0 + gate * (1.0 - sigmoid_gate))
        factors[2] = silu_gate


def forward(inputs, w_gate, w_up, w_down):
    slots, width = inputs.shape
    hidden = w_gate.shape[0]
    pad = -(-hidden // 32) * 32
    steps = 4
    piece = lambda rows: pl.BlockSpec((rows, width // steps), lambda i: (0, i))
    return pl.pallas_call(
        forward_kernel,
        grid=(steps,),
        in_specs=[piece(slots), piece(hidden), piece(hidden), piece(hidden)],
        out_specs=[piece(2 * pad), piece(pad), pl.BlockSpec((3, slots, pad), lambda i: (0, 0, 0))],
        out_shape=[
            jax.ShapeDtypeStruct((2 * pad, width), BF16),
            jax.ShapeDtypeStruct((pad, width), BF16),
            jax.ShapeDtypeStruct((3, slots, pad), F32),
        ],
        scratch_shapes=[pltpu.VMEM((slots, 2 * pad), F32)],
        compiler_params=params(32),
        cost_estimate=pl.CostEstimate(
            flops=4 * slots * hidden * width,
            bytes_accessed=4 * width * (slots + 3 * hidden),
            transcendentals=0,
        ),
        name="forward",
    )(inputs, w_gate, w_up, w_down)


def pack_sums(total):
    high = total.astype(BF16).astype(F32)
    return jnp.where(iota(total.shape, 1) < LANES // 2, high, total - high).astype(BF16)


def unpack_sums(packed):
    return packed + pltpu.roll(packed, LANES // 2, axis=1)


def cut(source, first, width, lane):
    done = 0
    while done < width:
        src, dst = first + done, lane + done
        take = min(width - done, LANES - src % LANES, LANES - dst % LANES)
        shift = (dst - src) % LANES
        values = source(src // LANES)
        if shift:
            values = pltpu.roll(values, shift, axis=1)
        yield dst // LANES, dst % LANES, dst % LANES + take, values
        done += take


def slot_grads_kernel(
    capacity, expert, grads, down, factors, scale, both, out, held
):
    contract = (((1,), (1,)), ((), ()))
    peers, slots, pad = grads.shape[0], scale.shape[0], down.shape[0]
    part = down.shape[1] // peers
    back = jnp.zeros((slots, pad), F32)
    for peer in range(peers):
        columns = slice(peer * part, (peer + 1) * part)
        tiles = [grads[peer, j * slots : (j + 1) * slots, :] for j in range(part // LANES)]
        back = back + lax.dot_general(
            jnp.concatenate(tiles, axis=1), down[:, columns], contract, preferred_element_type=F32
        )
    sums = jnp.sum(factors[0] * back, axis=1, keepdims=True)
    scaled = scale[:, :1] * back
    d_gate, d_up = (scaled * factors[1]).astype(BF16), (scaled * factors[2]).astype(BF16)
    d_both = jnp.concatenate([d_gate, d_up], axis=1)

    experts = slots // capacity
    grid = jnp.where(iota((slots, LANES), 1) % (LANES // 2) == iota((slots, LANES), 0) % experts, sums, 0.0)
    rows = [jnp.sum(grid[c * experts : (c + 1) * experts], axis=0, keepdims=True) for c in range(capacity)]
    total = jnp.zeros((PAD, LANES), F32)
    for c, line in enumerate(rows):
        total = jnp.where(iota((PAD, LANES), 0) == c, line, total)
    packed = pack_sums(total)

    block = both.shape[1] // SIDE
    tiles = block // LANES
    share = block // SIDE
    for y in range(SIDE):
        columns = slice(y * block, (y + 1) * block)
        held[:, columns] = dot(d_both, both[:, columns]).astype(held.dtype)
    for peer in range(SIDE):
        out[peer, tiles * slots :, :] = packed

    def tile_of(tile):
        return held[:, tile * LANES : (tile + 1) * LANES]

    @pl.when(expert[0] % 2 == 0)
    def _():
        lane = iota((slots, LANES), 1)
        for x in range(SIDE):
            made = [None] * tiles
            for y in range(SIDE):
                for tile, low, high, values in cut(tile_of, y * block + x * share, share, y * share):
                    if made[tile] is None:
                        made[tile] = values
                    else:
                        made[tile] = jnp.where((lane >= low) & (lane < high), values, made[tile])
            for j in range(tiles):
                out[x, j * slots : (j + 1) * slots, :] = made[j].astype(BF16)

    @pl.when(expert[0] % 2 == 1)
    def _():
        for y in range(SIDE):
            for j in range(tiles):
                out[y, j * slots : (j + 1) * slots, :] = tile_of(y * tiles + j).astype(BF16)


def slot_grads(expert, grads, down, factors, scale, both, capacity):
    slots = scale.shape[0]
    width = both.shape[1]
    rows = width // SIDE // LANES * slots + PAD

    def body(*refs):
        slot_grads_kernel(capacity, *refs)

    return pl.pallas_call(
        body,
        in_specs=[smem()] + [vmem()] * 5,
        out_specs=vmem(),
        out_shape=jax.ShapeDtypeStruct((SIDE, rows, LANES), BF16),
        scratch_shapes=[pltpu.VMEM((slots, width), HELD)],
        compiler_params=params(32),
        name="slot_grads",
    )(expert, grads, down, factors, scale, both)


def total(recv, first, count):
    sums = recv[0, first : first + count].astype(F32)
    for peer in range(1, recv.shape[0]):
        sums = sums + recv[peer, first : first + count].astype(F32)
    return sums


def fold(slots, share):
    spare = LANES - share
    parts = share // spare
    rest = slots // (parts + 1)
    return spare, parts, rest


def first_sum_kernel(slots, recv, out):
    peers, rows, _ = recv.shape
    tiles = (rows - PAD) // slots
    share = tiles * LANES // peers
    spare, parts, rest = fold(slots, share)
    kept = slots - rest
    columns = [total(recv, j * slots, slots) for j in range(tiles)]
    sums = unpack_sums(total(recv, tiles * slots, PAD))
    half = PAD // 2
    packed = pack_sums(sums[:half] + pltpu.roll(sums[half:], LANES // 4, axis=1)).astype(F32)
    lane = iota((slots, LANES), 1)
    for peer in range(peers):
        made = None
        for _, low, high, values in cut(lambda tile: columns[tile], peer * share, share, 0):
            made = values if made is None else jnp.where((lane >= low) & (lane < high), values, made)
        last = [pltpu.roll(made[kept:], share - q * spare, axis=1) for q in range(parts)]
        grads = jnp.where(lane[:kept] < share, made[:kept], jnp.concatenate(last, axis=0))
        out[peer] = jnp.concatenate([grads, packed], axis=0).astype(BF16)


def first_sum(recv, slots, share):
    kept = slots - fold(slots, share)[2]

    def body(*refs):
        first_sum_kernel(slots, *refs)

    return pl.pallas_call(
        body,
        in_specs=[vmem()],
        out_specs=vmem(),
        out_shape=jax.ShapeDtypeStruct((SIDE, kept + PAD // 2, LANES), BF16),
        compiler_params=params(32),
        name="first_sum",
    )(recv)


def second_sum_kernel(slots, share, recv, out):
    rows = out.shape[0]
    experts = rows // PAD
    spare, parts, rest = fold(slots, share)
    kept = slots - rest
    sums = total(recv, 0, recv.shape[1])
    side = iota((rest, LANES), 1)
    last = jnp.zeros((rest, LANES), F32)
    for q in range(parts):
        piece = pltpu.roll(sums[q * rest : (q + 1) * rest], (q + 1) * spare, axis=1)
        last = jnp.where((side >= q * spare) & (side < (q + 1) * spare), piece, last)
    grads = jnp.concatenate([sums[:kept], last], axis=0)
    probs = unpack_sums(sums[kept:])
    probs = jnp.concatenate([probs, pltpu.roll(probs, LANES - LANES // 4, axis=1)], axis=0)
    line = dot(one_hot(iota((slots, PAD), 0) // experts == iota((slots, PAD), 1)), probs.astype(BF16))
    lane, row = iota((slots, LANES), 1), iota((slots, LANES), 0)
    column = jnp.sum(jnp.where(lane == row % experts, line, 0.0), axis=1, keepdims=True)
    values = jnp.where(lane < share, grads, jnp.where(lane == share, column, 0.0)).astype(BF16)
    out[...] = swap(jnp.concatenate([values, jnp.zeros((rows - slots, LANES), BF16)], axis=0))


def second_sum(recv, slots, share, experts):
    def body(*refs):
        second_sum_kernel(slots, share, *refs)

    return pl.pallas_call(
        body,
        in_specs=[vmem()],
        out_specs=vmem(),
        out_shape=jax.ShapeDtypeStruct((experts * PAD, LANES), BF16),
        compiler_params=params(32),
        name="second_sum",
    )(recv)


def combine_kernel(routes, picker, recv, in_grad, prob_grad):
    share = in_grad.shape[1]
    hot = picker[...]
    values = swap(recv[...])[: hot.shape[0]]
    summed = lax.dot_general(hot, values, (((0,), (0,)), ((), ())), preferred_element_type=F32)
    in_grad[...] = summed[:, :share].astype(BF16)
    column = values[:, share : share + 1].astype(F32)
    found = jnp.where(hot.astype(F32) > 0.0, column, 0.0)
    expert = iota(hot.shape, 0) % PAD
    for k in range(routes.shape[0]):
        hit = routes[k : k + 1, :] == expert
        prob_grad[k : k + 1, :] = jnp.sum(jnp.where(hit, found, 0.0), axis=0, keepdims=True)


def combine(routes, picker, recv, share):
    choices, tokens = routes.shape
    return pl.pallas_call(
        combine_kernel,
        in_specs=[vmem()] * 3,
        out_specs=[vmem()] * 2,
        out_shape=[
            jax.ShapeDtypeStruct((tokens, share), BF16),
            jax.ShapeDtypeStruct((choices, tokens), F32),
        ],
        compiler_params=params(32),
        name="combine",
    )(routes, picker, recv)


def exchange(values):
    return lax.all_to_all(values, "expert", split_axis=0, concat_axis=0, tiled=True)


def exchange_in_plane(values, even_along_x):
    experts = lax.axis_size("expert")
    groups = []
    for expert in range(experts):
        along_x = (expert % 2 == 0) == even_along_x
        for line in range(SIDE):
            group = [(line, i) if along_x else (i, line) for i in range(SIDE)]
            groups.append([(y * SIDE + x) * experts + expert for y, x in group])
    return lax.all_to_all(
        values, ("y", "x", "expert"), split_axis=0, concat_axis=0, axis_index_groups=groups, tiled=True
    )


def on_device(routes, probs, out_grad, saved_inputs, w_gate, w_up, w_down):
    experts = lax.axis_size("expert")
    capacity = saved_inputs.shape[2]
    width = out_grad.shape[1]
    share = width // (SIDE * SIDE)
    slots = experts * capacity
    routes = routes.T
    probs = probs.T
    at_x, at_y, expert = (
        lax.axis_index(axis).astype(jnp.int32).reshape(1) for axis in ("x", "y", "expert")
    )

    send, picker = pick(at_x, at_y, expert, routes, probs, out_grad, capacity, experts)
    recv = exchange(send.reshape(experts, -1, LANES)).reshape(-1, LANES)
    inputs = saved_inputs[0].transpose(1, 0, 2).reshape(slots, width)
    both, down, factors = forward(inputs, w_gate[0], w_up[0], w_down[0])

    shards, scale = spread(recv, both, width // SIDE, capacity)
    grads = exchange_in_plane(shards, True)
    parts = slot_grads(expert, grads, down, factors, scale, both, capacity)
    first = first_sum(exchange_in_plane(parts, True), slots, share)
    back = second_sum(exchange_in_plane(first, False), slots, share, experts)
    got = exchange(back.reshape(experts, PAD, LANES)).reshape(experts * PAD, LANES)
    in_grad, prob_grad = combine(routes, picker, got, share)
    return in_grad, prob_grad.T


def solution(mesh):
    grid = Mesh(mesh.devices.reshape(SIDE, SIDE, -1), ("y", "x", "expert"))
    dp = ("y", "x")
    placed = (
        P("expert", None),
        P("expert", None),
        P("expert", None),
        P("expert", None, None, None),
        P("expert", dp, None),
        P("expert", dp, None),
        P("expert", dp, None),
    )
    return jax.shard_map(
        on_device,
        mesh=grid,
        in_specs=placed,
        out_specs=(P("expert", dp), P("expert", None)),
        check_vma=False,
    )
```

```python
import jax
import jax.numpy as jnp
from jax import lax
from jax.experimental import pallas as pl
from jax.experimental.pallas import tpu as pltpu
from jax.sharding import Mesh
from jax.sharding import PartitionSpec as P

F32 = jnp.float32
BF16 = jnp.bfloat16
LANES = 128
PAD = 16
SIDE = 8
MIB = 1024 * 1024
HELD = jnp.bfloat16


def iota(shape, dim):
    return lax.broadcasted_iota(jnp.int32, shape, dim)


def one_hot(mask):
    return jnp.where(mask, 1.0, 0.0).astype(BF16)


def dot(a, b):
    return jnp.dot(a, b, preferred_element_type=F32)


def swap(values):
    row, source = iota((PAD * PAD, PAD * PAD), 0), iota((PAD * PAD, PAD * PAD), 1)
    order = one_hot(source == (row % PAD) * PAD + row // PAD)
    return dot(order, values).astype(values.dtype)


def params(mib):
    return pltpu.CompilerParams(vmem_limit_bytes=mib * MIB)


def vmem():
    return pl.BlockSpec(memory_space=pltpu.VMEM)


def hbm():
    return pl.BlockSpec(memory_space=pltpu.HBM)


def smem():
    return pl.BlockSpec(memory_space=pltpu.SMEM)


def pick_kernel(
    capacity, at_x, at_y, _, routes_in, probs_in, out_grad, send, picker, routes, probs, grad_x, grad_y, sems
):
    slots, tokens = picker.shape
    experts = slots // capacity
    tiles = grad_x.shape[1] // LANES
    copies = [
        pltpu.make_async_copy(routes_in, routes, sems.at[0]),
        pltpu.make_async_copy(probs_in, probs, sems.at[1]),
    ]
    for axis, (at, grad) in enumerate(((at_x, grad_x), (at_y, grad_y))):
        width = grad.shape[1]
        first = pl.multiple_of(at[0] * width, LANES)
        copies.append(
            pltpu.make_async_copy(out_grad.at[:, pl.ds(first, width)], grad, sems.at[2 + axis])
        )
    for copy in copies:
        copy.start()
    copies[0].wait()
    copies[1].wait()
    row = iota((slots, tokens), 0)
    expert, slot = row % experts, row // experts
    named = jnp.zeros((slots, tokens), F32)
    weight = jnp.zeros((slots, tokens), F32)
    rounded = probs[...].astype(BF16).astype(F32)
    for k in range(routes.shape[0]):
        hit = routes[k : k + 1, :] == expert
        named = named + jnp.where(hit, 1.0, 0.0)
        weight = weight + jnp.where(hit, rounded[k : k + 1, :], 0.0)
    earlier = one_hot(iota((tokens, tokens), 0) < iota((tokens, tokens), 1))
    before = dot(named.astype(BF16), earlier)
    chosen = (named > 0.0) & (before == slot.astype(F32))
    hot = one_hot(chosen)
    picker[...] = hot
    scale = jnp.sum(jnp.where(chosen, weight, 0.0), axis=1, keepdims=True)
    lane = iota((experts, LANES), 1)
    weights = jnp.zeros((experts, LANES), F32)
    for c in range(capacity):
        weights = jnp.where(lane == c, scale[c * experts : (c + 1) * experts], weights)
    copies[2].wait()
    copies[3].wait()
    even = iota((slots, LANES), 0) % 2 == 0
    pieces = []
    for j in range(tiles):
        columns = slice(j * LANES, (j + 1) * LANES)
        picked = jnp.where(even, dot(hot, grad_x[:, columns]), dot(hot, grad_y[:, columns]))
        pieces.append(picked.astype(BF16))
    chunk = send.shape[0] // experts
    spare = chunk - tiles * capacity - 1
    pieces += [weights.astype(BF16), jnp.zeros((spare * experts, LANES), BF16)]
    rows = jnp.concatenate(pieces, axis=0)
    for g in range(chunk // PAD):
        group = swap(rows[g * PAD * PAD : (g + 1) * PAD * PAD])
        for e in range(experts):
            send[e * chunk + g * PAD : e * chunk + (g + 1) * PAD, :] = group[e * PAD : (e + 1) * PAD]


def pick(at_x, at_y, expert, routes, probs, out_grad, capacity, experts):
    tokens, width = out_grad.shape
    part = width // SIDE
    choices = routes.shape[0]
    chunk = -(-(part // LANES * capacity + 1) // PAD) * PAD

    def body(*refs):
        pick_kernel(capacity, *refs)

    return pl.pallas_call(
        body,
        in_specs=[smem(), smem(), smem(), hbm(), hbm(), hbm()],
        out_specs=[vmem()] * 2,
        out_shape=[
            jax.ShapeDtypeStruct((experts * chunk, LANES), BF16),
            jax.ShapeDtypeStruct((experts * capacity, tokens), BF16),
        ],
        scratch_shapes=[
            pltpu.VMEM((choices, tokens), jnp.int32),
            pltpu.VMEM((choices, tokens), F32),
            pltpu.VMEM((tokens, part), BF16),
            pltpu.VMEM((tokens, part), BF16),
            pltpu.SemaphoreType.DMA((4,)),
        ],
        compiler_params=params(63),
        name="pick",
    )(at_x, at_y, expert, routes, probs, out_grad)


def spread_kernel(capacity, recv, after, out, scale):
    chunk = recv.shape[0] // PAD
    moved = []
    for g in range(chunk // PAD):
        group = [recv[s * chunk + g * PAD : s * chunk + (g + 1) * PAD, :] for s in range(PAD)]
        moved.append(swap(jnp.concatenate(group, axis=0)))
    rows = jnp.concatenate(moved, axis=0)
    kept = out.shape[1]
    for peer in range(out.shape[0]):
        out[peer] = rows[:kept]
    weights = rows[kept : kept + PAD].astype(F32)
    for c in range(capacity):
        column = jnp.broadcast_to(weights[:, c : c + 1], (PAD, LANES))
        scale[c * PAD : (c + 1) * PAD, :] = column


def spread(recv, after, part, capacity):
    slots = PAD * capacity
    kept = part // LANES * slots

    def body(*refs):
        spread_kernel(capacity, *refs)

    return pl.pallas_call(
        body,
        in_specs=[vmem(), pl.BlockSpec(memory_space=pl.ANY)],
        out_specs=[vmem(), vmem()],
        out_shape=[
            jax.ShapeDtypeStruct((SIDE, kept, LANES), BF16),
            jax.ShapeDtypeStruct((slots, LANES), F32),
        ],
        compiler_params=params(32),
        name="spread",
    )(recv, after)


def forward_kernel(inputs, gate_in, up_in, factors, gate_pre, up_pre):
    contract = (((1,), (1,)), ((), ()))
    step = pl.program_id(0)
    x = inputs[...]
    gate_part = lax.dot_general(x, gate_in[...], contract, preferred_element_type=F32)
    up_part = lax.dot_general(x, up_in[...], contract, preferred_element_type=F32)

    @pl.when(step == 0)
    def _():
        gate_pre[...] = gate_part
        up_pre[...] = up_part

    @pl.when(step > 0)
    def _():
        gate_pre[...] += gate_part
        up_pre[...] += up_part

    @pl.when(step == pl.num_programs(0) - 1)
    def _():
        gate, up = gate_pre[...], up_pre[...]
        sigmoid_gate = jax.nn.sigmoid(gate)
        silu_gate = gate * sigmoid_gate
        factors[0] = (silu_gate * up).astype(BF16).astype(F32)
        factors[1] = up * sigmoid_gate * (1.0 + gate * (1.0 - sigmoid_gate))
        factors[2] = silu_gate


def forward(inputs, w_gate, w_up):
    slots, width = inputs.shape
    hidden = w_gate.shape[0]
    steps = 4
    piece = lambda rows: pl.BlockSpec((rows, width // steps), lambda i: (0, i))
    return pl.pallas_call(
        forward_kernel,
        grid=(steps,),
        in_specs=[piece(slots), piece(hidden), piece(hidden)],
        out_specs=pl.BlockSpec((3, slots, hidden), lambda i: (0, 0, 0)),
        out_shape=jax.ShapeDtypeStruct((3, slots, hidden), F32),
        scratch_shapes=[pltpu.VMEM((slots, hidden), F32)] * 2,
        compiler_params=params(32),
        cost_estimate=pl.CostEstimate(
            flops=4 * slots * hidden * width,
            bytes_accessed=4 * width * (slots + 2 * hidden),
            transcendentals=0,
        ),
        name="forward",
    )(inputs, w_gate, w_up)


def pack_sums(total):
    high = total.astype(BF16).astype(F32)
    return jnp.where(iota(total.shape, 1) < LANES // 2, high, total - high).astype(BF16)


def unpack_sums(packed):
    return packed + pltpu.roll(packed, LANES // 2, axis=1)


def cut(source, first, width, lane):
    done = 0
    while done < width:
        src, dst = first + done, lane + done
        take = min(width - done, LANES - src % LANES, LANES - dst % LANES)
        shift = (dst - src) % LANES
        values = source(src // LANES)
        if shift:
            values = pltpu.roll(values, shift, axis=1)
        yield dst // LANES, dst % LANES, dst % LANES + take, values
        done += take


def slot_grads_kernel(
    capacity, expert, grads, down, factors, scale, w_gate, w_up, out, held
):
    contract = (((1,), (1,)), ((), ()))
    peers, slots, pad = grads.shape[0], scale.shape[0], down.shape[0]
    part = down.shape[1] // peers
    back = jnp.zeros((slots, pad), F32)
    for peer in range(peers):
        columns = slice(peer * part, (peer + 1) * part)
        tiles = [grads[peer, j * slots : (j + 1) * slots, :] for j in range(part // LANES)]
        back = back + lax.dot_general(
            jnp.concatenate(tiles, axis=1), down[:, columns], contract, preferred_element_type=F32
        )
    sums = jnp.sum(factors[0] * back, axis=1, keepdims=True)
    scaled = scale[:, :1] * back
    d_gate, d_up = (scaled * factors[1]).astype(BF16), (scaled * factors[2]).astype(BF16)

    experts = slots // capacity
    grid = jnp.where(iota((slots, LANES), 1) % (LANES // 2) == iota((slots, LANES), 0) % experts, sums, 0.0)
    rows = [jnp.sum(grid[c * experts : (c + 1) * experts], axis=0, keepdims=True) for c in range(capacity)]
    total = jnp.zeros((PAD, LANES), F32)
    for c, line in enumerate(rows):
        total = jnp.where(iota((PAD, LANES), 0) == c, line, total)
    packed = pack_sums(total)

    block = w_gate.shape[1] // SIDE
    tiles = block // LANES
    share = block // SIDE
    for y in range(SIDE):
        columns = slice(y * block, (y + 1) * block)
        grad = dot(d_gate, w_gate[:, columns]) + dot(d_up, w_up[:, columns])
        held[:, columns] = grad.astype(held.dtype)
    for peer in range(SIDE):
        out[peer, tiles * slots :, :] = packed

    def tile_of(tile):
        return held[:, tile * LANES : (tile + 1) * LANES]

    @pl.when(expert[0] % 2 == 0)
    def _():
        lane = iota((slots, LANES), 1)
        for x in range(SIDE):
            made = [None] * tiles
            for y in range(SIDE):
                for tile, low, high, values in cut(tile_of, y * block + x * share, share, y * share):
                    if made[tile] is None:
                        made[tile] = values
                    else:
                        made[tile] = jnp.where((lane >= low) & (lane < high), values, made[tile])
            for j in range(tiles):
                out[x, j * slots : (j + 1) * slots, :] = made[j].astype(BF16)

    @pl.when(expert[0] % 2 == 1)
    def _():
        for y in range(SIDE):
            for j in range(tiles):
                out[y, j * slots : (j + 1) * slots, :] = tile_of(y * tiles + j).astype(BF16)


def slot_grads(expert, grads, down, factors, scale, w_gate, w_up, capacity):
    slots = scale.shape[0]
    width = w_gate.shape[1]
    rows = width // SIDE // LANES * slots + PAD

    def body(*refs):
        slot_grads_kernel(capacity, *refs)

    return pl.pallas_call(
        body,
        in_specs=[smem()] + [vmem()] * 6,
        out_specs=vmem(),
        out_shape=jax.ShapeDtypeStruct((SIDE, rows, LANES), BF16),
        scratch_shapes=[pltpu.VMEM((slots, width), HELD)],
        compiler_params=params(32),
        name="slot_grads",
    )(expert, grads, down, factors, scale, w_gate, w_up)


def total(recv, first, count):
    sums = recv[0, first : first + count].astype(F32)
    for peer in range(1, recv.shape[0]):
        sums = sums + recv[peer, first : first + count].astype(F32)
    return sums


def fold(slots, share):
    spare = LANES - share
    parts = share // spare
    rest = slots // (parts + 1)
    return spare, parts, rest


def first_sum_kernel(slots, recv, out):
    peers, rows, _ = recv.shape
    tiles = (rows - PAD) // slots
    share = tiles * LANES // peers
    spare, parts, rest = fold(slots, share)
    kept = slots - rest
    columns = [total(recv, j * slots, slots) for j in range(tiles)]
    sums = unpack_sums(total(recv, tiles * slots, PAD))
    half = PAD // 2
    packed = pack_sums(sums[:half] + pltpu.roll(sums[half:], LANES // 4, axis=1)).astype(F32)
    lane = iota((slots, LANES), 1)
    for peer in range(peers):
        made = None
        for _, low, high, values in cut(lambda tile: columns[tile], peer * share, share, 0):
            made = values if made is None else jnp.where((lane >= low) & (lane < high), values, made)
        last = [pltpu.roll(made[kept:], share - q * spare, axis=1) for q in range(parts)]
        grads = jnp.where(lane[:kept] < share, made[:kept], jnp.concatenate(last, axis=0))
        out[peer] = jnp.concatenate([grads, packed], axis=0).astype(BF16)


def first_sum(recv, slots, share):
    kept = slots - fold(slots, share)[2]

    def body(*refs):
        first_sum_kernel(slots, *refs)

    return pl.pallas_call(
        body,
        in_specs=[vmem()],
        out_specs=vmem(),
        out_shape=jax.ShapeDtypeStruct((SIDE, kept + PAD // 2, LANES), BF16),
        compiler_params=params(32),
        name="first_sum",
    )(recv)


def second_sum_kernel(slots, share, recv, out):
    rows = out.shape[0]
    experts = rows // PAD
    spare, parts, rest = fold(slots, share)
    kept = slots - rest
    sums = total(recv, 0, recv.shape[1])
    side = iota((rest, LANES), 1)
    last = jnp.zeros((rest, LANES), F32)
    for q in range(parts):
        piece = pltpu.roll(sums[q * rest : (q + 1) * rest], (q + 1) * spare, axis=1)
        last = jnp.where((side >= q * spare) & (side < (q + 1) * spare), piece, last)
    grads = jnp.concatenate([sums[:kept], last], axis=0)
    probs = unpack_sums(sums[kept:])
    probs = jnp.concatenate([probs, pltpu.roll(probs, LANES - LANES // 4, axis=1)], axis=0)
    line = dot(one_hot(iota((slots, PAD), 0) // experts == iota((slots, PAD), 1)), probs.astype(BF16))
    lane, row = iota((slots, LANES), 1), iota((slots, LANES), 0)
    column = jnp.sum(jnp.where(lane == row % experts, line, 0.0), axis=1, keepdims=True)
    values = jnp.where(lane < share, grads, jnp.where(lane == share, column, 0.0)).astype(BF16)
    out[...] = swap(jnp.concatenate([values, jnp.zeros((rows - slots, LANES), BF16)], axis=0))


def second_sum(recv, slots, share, experts):
    def body(*refs):
        second_sum_kernel(slots, share, *refs)

    return pl.pallas_call(
        body,
        in_specs=[vmem()],
        out_specs=vmem(),
        out_shape=jax.ShapeDtypeStruct((experts * PAD, LANES), BF16),
        compiler_params=params(32),
        name="second_sum",
    )(recv)


def combine_kernel(routes, picker, recv, in_grad, prob_grad):
    share = in_grad.shape[1]
    hot = picker[...]
    values = swap(recv[...])[: hot.shape[0]]
    summed = lax.dot_general(hot, values, (((0,), (0,)), ((), ())), preferred_element_type=F32)
    in_grad[...] = summed[:, :share].astype(BF16)
    column = values[:, share : share + 1].astype(F32)
    found = jnp.where(hot.astype(F32) > 0.0, column, 0.0)
    expert = iota(hot.shape, 0) % PAD
    for k in range(routes.shape[0]):
        hit = routes[k : k + 1, :] == expert
        prob_grad[k : k + 1, :] = jnp.sum(jnp.where(hit, found, 0.0), axis=0, keepdims=True)


def combine(routes, picker, recv, share):
    choices, tokens = routes.shape
    return pl.pallas_call(
        combine_kernel,
        in_specs=[vmem()] * 3,
        out_specs=[vmem()] * 2,
        out_shape=[
            jax.ShapeDtypeStruct((tokens, share), BF16),
            jax.ShapeDtypeStruct((choices, tokens), F32),
        ],
        compiler_params=params(32),
        name="combine",
    )(routes, picker, recv)


def exchange(values):
    return lax.all_to_all(values, "expert", split_axis=0, concat_axis=0, tiled=True)


def exchange_in_plane(values, even_along_x):
    experts = lax.axis_size("expert")
    groups = []
    for expert in range(experts):
        along_x = (expert % 2 == 0) == even_along_x
        for line in range(SIDE):
            group = [(line, i) if along_x else (i, line) for i in range(SIDE)]
            groups.append([(y * SIDE + x) * experts + expert for y, x in group])
    return lax.all_to_all(
        values, ("y", "x", "expert"), split_axis=0, concat_axis=0, axis_index_groups=groups, tiled=True
    )


def on_device(routes, probs, out_grad, saved_inputs, w_gate, w_up, w_down):
    experts = lax.axis_size("expert")
    capacity = saved_inputs.shape[2]
    width = out_grad.shape[1]
    share = width // (SIDE * SIDE)
    slots = experts * capacity
    routes = routes.T
    probs = probs.T
    at_x, at_y, expert = (
        lax.axis_index(axis).astype(jnp.int32).reshape(1) for axis in ("x", "y", "expert")
    )

    send, picker = pick(at_x, at_y, expert, routes, probs, out_grad, capacity, experts)
    recv = exchange(send.reshape(experts, -1, LANES)).reshape(-1, LANES)
    inputs = saved_inputs[0].transpose(1, 0, 2).reshape(slots, width)
    factors = forward(inputs, w_gate[0], w_up[0])

    shards, scale = spread(recv, factors, width // SIDE, capacity)
    grads = exchange_in_plane(shards, True)
    parts = slot_grads(
        expert, grads, w_down[0], factors, scale, w_gate[0], w_up[0], capacity
    )
    first = first_sum(exchange_in_plane(parts, True), slots, share)
    back = second_sum(exchange_in_plane(first, False), slots, share, experts)
    got = exchange(back.reshape(experts, PAD, LANES)).reshape(experts * PAD, LANES)
    in_grad, prob_grad = combine(routes, picker, got, share)
    return in_grad, prob_grad.T


def solution(mesh):
    grid = Mesh(mesh.devices.reshape(SIDE, SIDE, -1), ("y", "x", "expert"))
    dp = ("y", "x")
    placed = (
        P("expert", None),
        P("expert", None),
        P("expert", None),
        P("expert", None, None, None),
        P("expert", dp, None),
        P("expert", dp, None),
        P("expert", dp, None),
    )
    return jax.shard_map(
        on_device,
        mesh=grid,
        in_specs=placed,
        out_specs=(P("expert", dp), P("expert", None)),
        check_vma=False,
    )
```

```python
import jax
import jax.numpy as jnp
from jax import lax
from jax.experimental import pallas as pl
from jax.experimental.pallas import tpu as pltpu
from jax.sharding import Mesh
from jax.sharding import PartitionSpec as P

F32 = jnp.float32
BF16 = jnp.bfloat16
LANES = 128
PAD = 16
SIDE = 8
MIB = 1024 * 1024
HELD = jnp.bfloat16


def iota(shape, dim):
    return lax.broadcasted_iota(jnp.int32, shape, dim)


def one_hot(mask):
    return jnp.where(mask, 1.0, 0.0).astype(BF16)


def dot(a, b):
    return jnp.dot(a, b, preferred_element_type=F32)


def swap(values):
    row, source = iota((PAD * PAD, PAD * PAD), 0), iota((PAD * PAD, PAD * PAD), 1)
    order = one_hot(source == (row % PAD) * PAD + row // PAD)
    return dot(order, values).astype(values.dtype)


def params(mib):
    return pltpu.CompilerParams(vmem_limit_bytes=mib * MIB)


def vmem():
    return pl.BlockSpec(memory_space=pltpu.VMEM)


def hbm():
    return pl.BlockSpec(memory_space=pltpu.HBM)


def smem():
    return pl.BlockSpec(memory_space=pltpu.SMEM)


def pick_kernel(
    capacity, at_x, at_y, _, routes_in, probs_in, out_grad, send, picker, routes, probs, grad_x, grad_y, sems
):
    slots, tokens = picker.shape
    experts = slots // capacity
    tiles = grad_x.shape[1] // LANES
    copies = [
        pltpu.make_async_copy(routes_in, routes, sems.at[0]),
        pltpu.make_async_copy(probs_in, probs, sems.at[1]),
    ]
    for axis, (at, grad) in enumerate(((at_x, grad_x), (at_y, grad_y))):
        width = grad.shape[1]
        first = pl.multiple_of(at[0] * width, LANES)
        copies.append(
            pltpu.make_async_copy(out_grad.at[:, pl.ds(first, width)], grad, sems.at[2 + axis])
        )
    for copy in copies:
        copy.start()
    copies[0].wait()
    copies[1].wait()
    row = iota((slots, tokens), 0)
    expert, slot = row % experts, row // experts
    named = jnp.zeros((slots, tokens), F32)
    weight = jnp.zeros((slots, tokens), F32)
    rounded = probs[...].astype(BF16).astype(F32)
    for k in range(routes.shape[0]):
        hit = routes[k : k + 1, :] == expert
        named = named + jnp.where(hit, 1.0, 0.0)
        weight = weight + jnp.where(hit, rounded[k : k + 1, :], 0.0)
    earlier = one_hot(iota((tokens, tokens), 0) < iota((tokens, tokens), 1))
    before = dot(named.astype(BF16), earlier)
    chosen = (named > 0.0) & (before == slot.astype(F32))
    hot = one_hot(chosen)
    picker[...] = hot
    scale = jnp.sum(jnp.where(chosen, weight, 0.0), axis=1, keepdims=True)
    lane = iota((experts, LANES), 1)
    weights = jnp.zeros((experts, LANES), F32)
    for c in range(capacity):
        weights = jnp.where(lane == c, scale[c * experts : (c + 1) * experts], weights)
    copies[2].wait()
    copies[3].wait()
    even = iota((slots, LANES), 0) % 2 == 0
    pieces = []
    for j in range(tiles):
        columns = slice(j * LANES, (j + 1) * LANES)
        picked = jnp.where(even, dot(hot, grad_x[:, columns]), dot(hot, grad_y[:, columns]))
        pieces.append(picked.astype(BF16))
    chunk = send.shape[0] // experts
    spare = chunk - tiles * capacity - 1
    pieces += [weights.astype(BF16), jnp.zeros((spare * experts, LANES), BF16)]
    rows = jnp.concatenate(pieces, axis=0)
    for g in range(chunk // PAD):
        group = swap(rows[g * PAD * PAD : (g + 1) * PAD * PAD])
        for e in range(experts):
            send[e * chunk + g * PAD : e * chunk + (g + 1) * PAD, :] = group[e * PAD : (e + 1) * PAD]


def pick(at_x, at_y, expert, routes, probs, out_grad, capacity, experts):
    tokens, width = out_grad.shape
    part = width // SIDE
    choices = routes.shape[0]
    chunk = -(-(part // LANES * capacity + 1) // PAD) * PAD

    def body(*refs):
        pick_kernel(capacity, *refs)

    return pl.pallas_call(
        body,
        in_specs=[smem(), smem(), smem(), hbm(), hbm(), hbm()],
        out_specs=[vmem()] * 2,
        out_shape=[
            jax.ShapeDtypeStruct((experts * chunk, LANES), BF16),
            jax.ShapeDtypeStruct((experts * capacity, tokens), BF16),
        ],
        scratch_shapes=[
            pltpu.VMEM((choices, tokens), jnp.int32),
            pltpu.VMEM((choices, tokens), F32),
            pltpu.VMEM((tokens, part), BF16),
            pltpu.VMEM((tokens, part), BF16),
            pltpu.SemaphoreType.DMA((4,)),
        ],
        compiler_params=params(63),
        name="pick",
    )(at_x, at_y, expert, routes, probs, out_grad)


def spread_kernel(capacity, recv, factors, down, out, scale):
    chunk = recv.shape[0] // PAD
    moved = []
    for g in range(chunk // PAD):
        group = [recv[s * chunk + g * PAD : s * chunk + (g + 1) * PAD, :] for s in range(PAD)]
        moved.append(swap(jnp.concatenate(group, axis=0)))
    rows = jnp.concatenate(moved, axis=0)
    kept = out.shape[1]
    for peer in range(out.shape[0]):
        out[peer] = rows[:kept]
    weights = rows[kept : kept + PAD].astype(F32)
    for c in range(capacity):
        column = jnp.broadcast_to(weights[:, c : c + 1], (PAD, LANES))
        scale[c * PAD : (c + 1) * PAD, :] = column


def spread(recv, factors, down, part, capacity):
    slots = PAD * capacity
    kept = part // LANES * slots

    def body(*refs):
        spread_kernel(capacity, *refs)

    return pl.pallas_call(
        body,
        in_specs=[vmem()] + [pl.BlockSpec(memory_space=pl.ANY)] * 2,
        out_specs=[vmem(), vmem()],
        out_shape=[
            jax.ShapeDtypeStruct((SIDE, kept, LANES), BF16),
            jax.ShapeDtypeStruct((slots, LANES), F32),
        ],
        compiler_params=params(32),
        name="spread",
    )(recv, factors, down)


def forward_kernel(inputs, gate_in, up_in, factors, gate_pre, up_pre):
    contract = (((1,), (1,)), ((), ()))
    step = pl.program_id(0)
    x = inputs[...]
    gate_part = lax.dot_general(x, gate_in[...], contract, preferred_element_type=F32)
    up_part = lax.dot_general(x, up_in[...], contract, preferred_element_type=F32)

    @pl.when(step == 0)
    def _():
        gate_pre[...] = gate_part
        up_pre[...] = up_part

    @pl.when(step > 0)
    def _():
        gate_pre[...] += gate_part
        up_pre[...] += up_part

    @pl.when(step == pl.num_programs(0) - 1)
    def _():
        gate, up = gate_pre[...], up_pre[...]
        sigmoid_gate = jax.nn.sigmoid(gate)
        silu_gate = gate * sigmoid_gate
        factors[0] = (silu_gate * up).astype(BF16).astype(F32)
        factors[1] = up * sigmoid_gate * (1.0 + gate * (1.0 - sigmoid_gate))
        factors[2] = silu_gate


def forward(inputs, w_gate, w_up):
    slots, width = inputs.shape
    hidden = w_gate.shape[0]
    steps = 4
    piece = lambda rows: pl.BlockSpec((rows, width // steps), lambda i: (0, i))
    return pl.pallas_call(
        forward_kernel,
        grid=(steps,),
        in_specs=[piece(slots), piece(hidden), piece(hidden)],
        out_specs=pl.BlockSpec((3, slots, hidden), lambda i: (0, 0, 0)),
        out_shape=jax.ShapeDtypeStruct((3, slots, hidden), F32),
        scratch_shapes=[pltpu.VMEM((slots, hidden), F32)] * 2,
        compiler_params=params(32),
        cost_estimate=pl.CostEstimate(
            flops=4 * slots * hidden * width,
            bytes_accessed=4 * width * (slots + 2 * hidden),
            transcendentals=0,
        ),
        name="forward",
    )(inputs, w_gate, w_up)


def pack_sums(total):
    high = total.astype(BF16).astype(F32)
    return jnp.where(iota(total.shape, 1) < LANES // 2, high, total - high).astype(BF16)


def unpack_sums(packed):
    return packed + pltpu.roll(packed, LANES // 2, axis=1)


def cut(source, first, width, lane):
    done = 0
    while done < width:
        src, dst = first + done, lane + done
        take = min(width - done, LANES - src % LANES, LANES - dst % LANES)
        shift = (dst - src) % LANES
        values = source(src // LANES)
        if shift:
            values = pltpu.roll(values, shift, axis=1)
        yield dst // LANES, dst % LANES, dst % LANES + take, values
        done += take


def slot_grads_kernel(
    capacity, expert, grads, down, factors, scale, w_gate, w_up, out, held
):
    peers, slots = grads.shape[0], scale.shape[0]
    part = down.shape[0] // peers
    tiles = [
        grads[peer, j * slots : (j + 1) * slots, :]
        for peer in range(peers)
        for j in range(part // LANES)
    ]
    back = dot(jnp.concatenate(tiles, axis=1), down[...])
    sums = jnp.sum(factors[0] * back, axis=1, keepdims=True)
    scaled = scale[:, :1] * back
    d_gate, d_up = (scaled * factors[1]).astype(BF16), (scaled * factors[2]).astype(BF16)

    d_both = jnp.concatenate([d_gate, d_up], axis=1)
    experts = slots // capacity
    grid = jnp.where(iota((slots, LANES), 1) % (LANES // 2) == iota((slots, LANES), 0) % experts, sums, 0.0)
    rows = [jnp.sum(grid[c * experts : (c + 1) * experts], axis=0, keepdims=True) for c in range(capacity)]
    total = jnp.zeros((PAD, LANES), F32)
    for c, line in enumerate(rows):
        total = jnp.where(iota((PAD, LANES), 0) == c, line, total)
    packed = pack_sums(total)

    block = w_gate.shape[1] // SIDE
    tiles = block // LANES
    share = block // SIDE
    for y in range(SIDE):
        columns = slice(y * block, (y + 1) * block)
        grad = dot(d_both, jnp.concatenate([w_gate[:, columns], w_up[:, columns]], axis=0))
        held[:, columns] = grad.astype(held.dtype)
    for peer in range(SIDE):
        out[peer, tiles * slots :, :] = packed

    def tile_of(tile):
        return held[:, tile * LANES : (tile + 1) * LANES]

    @pl.when(expert[0] % 2 == 0)
    def _():
        lane = iota((slots, LANES), 1)
        for x in range(SIDE):
            made = [None] * tiles
            for y in range(SIDE):
                for tile, low, high, values in cut(tile_of, y * block + x * share, share, y * share):
                    if made[tile] is None:
                        made[tile] = values
                    else:
                        made[tile] = jnp.where((lane >= low) & (lane < high), values, made[tile])
            for j in range(tiles):
                out[x, j * slots : (j + 1) * slots, :] = made[j].astype(BF16)

    @pl.when(expert[0] % 2 == 1)
    def _():
        for y in range(SIDE):
            for j in range(tiles):
                out[y, j * slots : (j + 1) * slots, :] = tile_of(y * tiles + j).astype(BF16)


def slot_grads(expert, grads, down, factors, scale, w_gate, w_up, capacity):
    slots = scale.shape[0]
    width = w_gate.shape[1]
    rows = width // SIDE // LANES * slots + PAD

    def body(*refs):
        slot_grads_kernel(capacity, *refs)

    return pl.pallas_call(
        body,
        in_specs=[smem()] + [vmem()] * 6,
        out_specs=vmem(),
        out_shape=jax.ShapeDtypeStruct((SIDE, rows, LANES), BF16),
        scratch_shapes=[pltpu.VMEM((slots, width), HELD)],
        compiler_params=params(32),
        name="slot_grads",
    )(expert, grads, down, factors, scale, w_gate, w_up)


def total(recv, first, count):
    sums = recv[0, first : first + count].astype(F32)
    for peer in range(1, recv.shape[0]):
        sums = sums + recv[peer, first : first + count].astype(F32)
    return sums


def fold(slots, share):
    spare = LANES - share
    parts = share // spare
    rest = slots // (parts + 1)
    return spare, parts, rest


def first_sum_kernel(slots, recv, out):
    peers, rows, _ = recv.shape
    tiles = (rows - PAD) // slots
    share = tiles * LANES // peers
    spare, parts, rest = fold(slots, share)
    kept = slots - rest
    columns = [total(recv, j * slots, slots) for j in range(tiles)]
    sums = unpack_sums(total(recv, tiles * slots, PAD))
    half = PAD // 2
    packed = pack_sums(sums[:half] + pltpu.roll(sums[half:], LANES // 4, axis=1)).astype(F32)
    lane = iota((slots, LANES), 1)
    for peer in range(peers):
        made = None
        for _, low, high, values in cut(lambda tile: columns[tile], peer * share, share, 0):
            made = values if made is None else jnp.where((lane >= low) & (lane < high), values, made)
        last = [pltpu.roll(made[kept:], share - q * spare, axis=1) for q in range(parts)]
        grads = jnp.where(lane[:kept] < share, made[:kept], jnp.concatenate(last, axis=0))
        out[peer] = jnp.concatenate([grads, packed], axis=0).astype(BF16)


def first_sum(recv, slots, share):
    kept = slots - fold(slots, share)[2]

    def body(*refs):
        first_sum_kernel(slots, *refs)

    return pl.pallas_call(
        body,
        in_specs=[vmem()],
        out_specs=vmem(),
        out_shape=jax.ShapeDtypeStruct((SIDE, kept + PAD // 2, LANES), BF16),
        compiler_params=params(32),
        name="first_sum",
    )(recv)


def second_sum_kernel(slots, share, recv, out):
    rows = out.shape[0]
    experts = rows // PAD
    spare, parts, rest = fold(slots, share)
    kept = slots - rest
    sums = total(recv, 0, recv.shape[1])
    side = iota((rest, LANES), 1)
    last = jnp.zeros((rest, LANES), F32)
    for q in range(parts):
        piece = pltpu.roll(sums[q * rest : (q + 1) * rest], (q + 1) * spare, axis=1)
        last = jnp.where((side >= q * spare) & (side < (q + 1) * spare), piece, last)
    grads = jnp.concatenate([sums[:kept], last], axis=0)
    probs = unpack_sums(sums[kept:])
    probs = jnp.concatenate([probs, pltpu.roll(probs, LANES - LANES // 4, axis=1)], axis=0)
    line = dot(one_hot(iota((slots, PAD), 0) // experts == iota((slots, PAD), 1)), probs.astype(BF16))
    lane, row = iota((slots, LANES), 1), iota((slots, LANES), 0)
    column = jnp.sum(jnp.where(lane == row % experts, line, 0.0), axis=1, keepdims=True)
    values = jnp.where(lane < share, grads, jnp.where(lane == share, column, 0.0)).astype(BF16)
    out[...] = swap(jnp.concatenate([values, jnp.zeros((rows - slots, LANES), BF16)], axis=0))


def second_sum(recv, slots, share, experts):
    def body(*refs):
        second_sum_kernel(slots, share, *refs)

    return pl.pallas_call(
        body,
        in_specs=[vmem()],
        out_specs=vmem(),
        out_shape=jax.ShapeDtypeStruct((experts * PAD, LANES), BF16),
        compiler_params=params(32),
        name="second_sum",
    )(recv)


def combine_kernel(routes, picker, recv, in_grad, prob_grad):
    share = in_grad.shape[1]
    hot = picker[...]
    values = swap(recv[...])[: hot.shape[0]]
    summed = lax.dot_general(hot, values, (((0,), (0,)), ((), ())), preferred_element_type=F32)
    in_grad[...] = summed[:, :share].astype(BF16)
    column = values[:, share : share + 1].astype(F32)
    found = jnp.where(hot.astype(F32) > 0.0, column, 0.0)
    expert = iota(hot.shape, 0) % PAD
    for k in range(routes.shape[0]):
        hit = routes[k : k + 1, :] == expert
        prob_grad[k : k + 1, :] = jnp.sum(jnp.where(hit, found, 0.0), axis=0, keepdims=True)


def combine(routes, picker, recv, share):
    choices, tokens = routes.shape
    return pl.pallas_call(
        combine_kernel,
        in_specs=[vmem()] * 3,
        out_specs=[vmem()] * 2,
        out_shape=[
            jax.ShapeDtypeStruct((tokens, share), BF16),
            jax.ShapeDtypeStruct((choices, tokens), F32),
        ],
        compiler_params=params(32),
        name="combine",
    )(routes, picker, recv)


def exchange(values):
    return lax.all_to_all(values, "expert", split_axis=0, concat_axis=0, tiled=True)


def exchange_in_plane(values, even_along_x):
    experts = lax.axis_size("expert")
    groups = []
    for expert in range(experts):
        along_x = (expert % 2 == 0) == even_along_x
        for line in range(SIDE):
            group = [(line, i) if along_x else (i, line) for i in range(SIDE)]
            groups.append([(y * SIDE + x) * experts + expert for y, x in group])
    return lax.all_to_all(
        values, ("y", "x", "expert"), split_axis=0, concat_axis=0, axis_index_groups=groups, tiled=True
    )


def on_device(routes, probs, out_grad, saved_inputs, w_gate, w_up, w_down):
    experts = lax.axis_size("expert")
    capacity = saved_inputs.shape[2]
    width = out_grad.shape[1]
    share = width // (SIDE * SIDE)
    slots = experts * capacity
    routes = routes.T
    probs = probs.T
    at_x, at_y, expert = (
        lax.axis_index(axis).astype(jnp.int32).reshape(1) for axis in ("x", "y", "expert")
    )

    send, picker = pick(at_x, at_y, expert, routes, probs, out_grad, capacity, experts)
    recv = exchange(send.reshape(experts, -1, LANES)).reshape(-1, LANES)
    inputs = saved_inputs[0].transpose(1, 0, 2).reshape(slots, width)
    factors = forward(inputs, w_gate[0], w_up[0])
    down = w_down[0].T

    shards, scale = spread(recv, factors, down, width // SIDE, capacity)
    grads = exchange_in_plane(shards, True)
    parts = slot_grads(
        expert, grads, down, factors, scale, w_gate[0], w_up[0], capacity
    )
    first = first_sum(exchange_in_plane(parts, True), slots, share)
    back = second_sum(exchange_in_plane(first, False), slots, share, experts)
    got = exchange(back.reshape(experts, PAD, LANES)).reshape(experts * PAD, LANES)
    in_grad, prob_grad = combine(routes, picker, got, share)
    return in_grad, prob_grad.T


def solution(mesh):
    grid = Mesh(mesh.devices.reshape(SIDE, SIDE, -1), ("y", "x", "expert"))
    dp = ("y", "x")
    placed = (
        P("expert", None),
        P("expert", None),
        P("expert", None),
        P("expert", None, None, None),
        P("expert", dp, None),
        P("expert", dp, None),
        P("expert", dp, None),
    )
    return jax.shard_map(
        on_device,
        mesh=grid,
        in_specs=placed,
        out_specs=(P("expert", dp), P("expert", None)),
        check_vma=False,
    )
```

```python
import jax
import jax.numpy as jnp
from jax import lax
from jax.experimental import pallas as pl
from jax.experimental.pallas import tpu as pltpu
from jax.sharding import Mesh
from jax.sharding import PartitionSpec as P

F32 = jnp.float32
BF16 = jnp.bfloat16
LANES = 128
PAD = 16
SIDE = 8
MIB = 1024 * 1024
HELD = jnp.bfloat16


def iota(shape, dim):
    return lax.broadcasted_iota(jnp.int32, shape, dim)


def one_hot(mask):
    return jnp.where(mask, 1.0, 0.0).astype(BF16)


def dot(a, b):
    return jnp.dot(a, b, preferred_element_type=F32)


def swap(values):
    row, source = iota((PAD * PAD, PAD * PAD), 0), iota((PAD * PAD, PAD * PAD), 1)
    order = one_hot(source == (row % PAD) * PAD + row // PAD)
    return dot(order, values).astype(values.dtype)


def params(mib):
    return pltpu.CompilerParams(vmem_limit_bytes=mib * MIB)


def vmem():
    return pl.BlockSpec(memory_space=pltpu.VMEM)


def hbm():
    return pl.BlockSpec(memory_space=pltpu.HBM)


def smem():
    return pl.BlockSpec(memory_space=pltpu.SMEM)


def pick_kernel(
    capacity, at_x, at_y, _, routes_in, probs_in, out_grad, send, picker, routes, probs, grad_x, grad_y, sems
):
    slots, tokens = picker.shape
    experts = slots // capacity
    tiles = grad_x.shape[1] // LANES
    copies = [
        pltpu.make_async_copy(routes_in, routes, sems.at[0]),
        pltpu.make_async_copy(probs_in, probs, sems.at[1]),
    ]
    for axis, (at, grad) in enumerate(((at_x, grad_x), (at_y, grad_y))):
        width = grad.shape[1]
        first = pl.multiple_of(at[0] * width, LANES)
        copies.append(
            pltpu.make_async_copy(out_grad.at[:, pl.ds(first, width)], grad, sems.at[2 + axis])
        )
    for copy in copies:
        copy.start()
    copies[0].wait()
    copies[1].wait()
    row = iota((slots, tokens), 0)
    expert, slot = row % experts, row // experts
    named = jnp.zeros((slots, tokens), F32)
    weight = jnp.zeros((slots, tokens), F32)
    rounded = probs[...].astype(BF16).astype(F32)
    for k in range(routes.shape[0]):
        hit = routes[k : k + 1, :] == expert
        named = named + jnp.where(hit, 1.0, 0.0)
        weight = weight + jnp.where(hit, rounded[k : k + 1, :], 0.0)
    earlier = one_hot(iota((tokens, tokens), 0) < iota((tokens, tokens), 1))
    before = dot(named.astype(BF16), earlier)
    chosen = (named > 0.0) & (before == slot.astype(F32))
    hot = one_hot(chosen)
    picker[...] = hot
    scale = jnp.sum(jnp.where(chosen, weight, 0.0), axis=1, keepdims=True)
    lane = iota((experts, LANES), 1)
    weights = jnp.zeros((experts, LANES), F32)
    for c in range(capacity):
        weights = jnp.where(lane == c, scale[c * experts : (c + 1) * experts], weights)
    copies[2].wait()
    copies[3].wait()
    even = iota((slots, LANES), 0) % 2 == 0
    pieces = []
    for j in range(tiles):
        columns = slice(j * LANES, (j + 1) * LANES)
        picked = jnp.where(even, dot(hot, grad_x[:, columns]), dot(hot, grad_y[:, columns]))
        pieces.append(picked.astype(BF16))
    chunk = send.shape[0] // experts
    spare = chunk - tiles * capacity - 1
    pieces += [weights.astype(BF16), jnp.zeros((spare * experts, LANES), BF16)]
    rows = jnp.concatenate(pieces, axis=0)
    for g in range(chunk // PAD):
        group = swap(rows[g * PAD * PAD : (g + 1) * PAD * PAD])
        for e in range(experts):
            send[e * chunk + g * PAD : e * chunk + (g + 1) * PAD, :] = group[e * PAD : (e + 1) * PAD]


def pick(at_x, at_y, expert, routes, probs, out_grad, capacity, experts):
    tokens, width = out_grad.shape
    part = width // SIDE
    choices = routes.shape[0]
    chunk = -(-(part // LANES * capacity + 1) // PAD) * PAD

    def body(*refs):
        pick_kernel(capacity, *refs)

    return pl.pallas_call(
        body,
        in_specs=[smem(), smem(), smem(), hbm(), hbm(), hbm()],
        out_specs=[vmem()] * 2,
        out_shape=[
            jax.ShapeDtypeStruct((experts * chunk, LANES), BF16),
            jax.ShapeDtypeStruct((experts * capacity, tokens), BF16),
        ],
        scratch_shapes=[
            pltpu.VMEM((choices, tokens), jnp.int32),
            pltpu.VMEM((choices, tokens), F32),
            pltpu.VMEM((tokens, part), BF16),
            pltpu.VMEM((tokens, part), BF16),
            pltpu.SemaphoreType.DMA((4,)),
        ],
        compiler_params=params(63),
        name="pick",
    )(at_x, at_y, expert, routes, probs, out_grad)


def spread_kernel(capacity, recv, factors, down, out, scale):
    chunk = recv.shape[0] // PAD
    moved = []
    for g in range(chunk // PAD):
        group = [recv[s * chunk + g * PAD : s * chunk + (g + 1) * PAD, :] for s in range(PAD)]
        moved.append(swap(jnp.concatenate(group, axis=0)))
    rows = jnp.concatenate(moved, axis=0)
    kept = out.shape[1]
    for peer in range(out.shape[0]):
        out[peer] = rows[:kept]
    weights = rows[kept : kept + PAD].astype(F32)
    for c in range(capacity):
        column = jnp.broadcast_to(weights[:, c : c + 1], (PAD, LANES))
        scale[c * PAD : (c + 1) * PAD, :] = column


def spread(recv, factors, down, part, capacity):
    slots = PAD * capacity
    kept = part // LANES * slots

    def body(*refs):
        spread_kernel(capacity, *refs)

    return pl.pallas_call(
        body,
        in_specs=[vmem()] + [pl.BlockSpec(memory_space=pl.ANY)] * 2,
        out_specs=[vmem(), vmem()],
        out_shape=[
            jax.ShapeDtypeStruct((SIDE, kept, LANES), BF16),
            jax.ShapeDtypeStruct((slots, LANES), F32),
        ],
        compiler_params=params(32),
        name="spread",
    )(recv, factors, down)


def forward_kernel(inputs, gate_in, up_in, factors, gate_pre, up_pre):
    contract = (((1,), (1,)), ((), ()))
    step = pl.program_id(0)
    x = inputs[...]
    gate_part = lax.dot_general(x, gate_in[...], contract, preferred_element_type=F32)
    up_part = lax.dot_general(x, up_in[...], contract, preferred_element_type=F32)

    @pl.when(step == 0)
    def _():
        gate_pre[...] = gate_part
        up_pre[...] = up_part

    @pl.when(step > 0)
    def _():
        gate_pre[...] += gate_part
        up_pre[...] += up_part

    @pl.when(step == pl.num_programs(0) - 1)
    def _():
        gate, up = gate_pre[...], up_pre[...]
        sigmoid_gate = jax.nn.sigmoid(gate)
        silu_gate = gate * sigmoid_gate
        factors[0] = (silu_gate * up).astype(BF16).astype(F32)
        factors[1] = up * sigmoid_gate * (1.0 + gate * (1.0 - sigmoid_gate))
        factors[2] = silu_gate


def forward(inputs, w_gate, w_up):
    slots, width = inputs.shape
    hidden = w_gate.shape[0]
    steps = 4
    piece = lambda rows: pl.BlockSpec((rows, width // steps), lambda i: (0, i))
    return pl.pallas_call(
        forward_kernel,
        grid=(steps,),
        in_specs=[piece(slots), piece(hidden), piece(hidden)],
        out_specs=pl.BlockSpec((3, slots, hidden), lambda i: (0, 0, 0)),
        out_shape=jax.ShapeDtypeStruct((3, slots, hidden), F32),
        scratch_shapes=[pltpu.VMEM((slots, hidden), F32)] * 2,
        compiler_params=params(32),
        cost_estimate=pl.CostEstimate(
            flops=4 * slots * hidden * width,
            bytes_accessed=4 * width * (slots + 2 * hidden),
            transcendentals=0,
        ),
        name="forward",
    )(inputs, w_gate, w_up)


def pack_sums(total):
    high = total.astype(BF16).astype(F32)
    return jnp.where(iota(total.shape, 1) < LANES // 2, high, total - high).astype(BF16)


def unpack_sums(packed):
    return packed + pltpu.roll(packed, LANES // 2, axis=1)


def cut(source, first, width, lane):
    done = 0
    while done < width:
        src, dst = first + done, lane + done
        take = min(width - done, LANES - src % LANES, LANES - dst % LANES)
        shift = (dst - src) % LANES
        values = source(src // LANES)
        if shift:
            values = pltpu.roll(values, shift, axis=1)
        yield dst // LANES, dst % LANES, dst % LANES + take, values
        done += take


def slot_grads_kernel(
    capacity, expert, grads, down, factors, scale, w_gate, w_up, out, held
):
    peers, slots = grads.shape[0], scale.shape[0]
    part = down.shape[0] // peers
    tiles = [
        grads[peer, j * slots : (j + 1) * slots, :]
        for peer in range(peers)
        for j in range(part // LANES)
    ]
    back = dot(jnp.concatenate(tiles, axis=1), down[...])
    sums = jnp.sum(factors[0] * back, axis=1, keepdims=True)
    scaled = scale[:, :1] * back
    d_gate, d_up = (scaled * factors[1]).astype(BF16), (scaled * factors[2]).astype(BF16)

    d_both = jnp.concatenate([d_gate, d_up], axis=1)
    experts = slots // capacity
    grid = jnp.where(iota((slots, LANES), 1) % (LANES // 2) == iota((slots, LANES), 0) % experts, sums, 0.0)
    rows = [jnp.sum(grid[c * experts : (c + 1) * experts], axis=0, keepdims=True) for c in range(capacity)]
    total = jnp.zeros((PAD, LANES), F32)
    for c, line in enumerate(rows):
        total = jnp.where(iota((PAD, LANES), 0) == c, line, total)
    packed = pack_sums(total)

    block = w_gate.shape[1] // SIDE
    tiles = block // LANES
    share = block // SIDE
    for y in range(SIDE):
        columns = slice(y * block, (y + 1) * block)
        grad = dot(d_both, jnp.concatenate([w_gate[:, columns], w_up[:, columns]], axis=0))
        held[:, columns] = grad.astype(held.dtype)
    for peer in range(SIDE):
        out[peer, tiles * slots :, :] = packed

    def tile_of(tile):
        return held[:, tile * LANES : (tile + 1) * LANES]

    @pl.when(expert[0] % 2 == 1)
    def _():
        lane = iota((slots, LANES), 1)
        for x in range(SIDE):
            made = [None] * tiles
            for y in range(SIDE):
                for tile, low, high, values in cut(tile_of, y * block + x * share, share, y * share):
                    if made[tile] is None:
                        made[tile] = values
                    else:
                        made[tile] = jnp.where((lane >= low) & (lane < high), values, made[tile])
            for j in range(tiles):
                out[x, j * slots : (j + 1) * slots, :] = made[j].astype(BF16)

    @pl.when(expert[0] % 2 == 0)
    def _():
        for y in range(SIDE):
            for j in range(tiles):
                out[y, j * slots : (j + 1) * slots, :] = tile_of(y * tiles + j).astype(BF16)


def slot_grads(expert, grads, down, factors, scale, w_gate, w_up, capacity):
    slots = scale.shape[0]
    width = w_gate.shape[1]
    rows = width // SIDE // LANES * slots + PAD

    def body(*refs):
        slot_grads_kernel(capacity, *refs)

    return pl.pallas_call(
        body,
        in_specs=[smem()] + [vmem()] * 6,
        out_specs=vmem(),
        out_shape=jax.ShapeDtypeStruct((SIDE, rows, LANES), BF16),
        scratch_shapes=[pltpu.VMEM((slots, width), HELD)],
        compiler_params=params(32),
        name="slot_grads",
    )(expert, grads, down, factors, scale, w_gate, w_up)


def total(recv, first, count):
    sums = recv[0, first : first + count].astype(F32)
    for peer in range(1, recv.shape[0]):
        sums = sums + recv[peer, first : first + count].astype(F32)
    return sums


def fold(slots, share):
    spare = LANES - share
    parts = share // spare
    rest = slots // (parts + 1)
    return spare, parts, rest


def first_sum_kernel(slots, recv, out):
    peers, rows, _ = recv.shape
    tiles = (rows - PAD) // slots
    share = tiles * LANES // peers
    spare, parts, rest = fold(slots, share)
    kept = slots - rest
    columns = [total(recv, j * slots, slots) for j in range(tiles)]
    sums = unpack_sums(total(recv, tiles * slots, PAD))
    half = PAD // 2
    packed = pack_sums(sums[:half] + pltpu.roll(sums[half:], LANES // 4, axis=1)).astype(F32)
    lane = iota((slots, LANES), 1)
    for peer in range(peers):
        made = None
        for _, low, high, values in cut(lambda tile: columns[tile], peer * share, share, 0):
            made = values if made is None else jnp.where((lane >= low) & (lane < high), values, made)
        last = [pltpu.roll(made[kept:], share - q * spare, axis=1) for q in range(parts)]
        grads = jnp.where(lane[:kept] < share, made[:kept], jnp.concatenate(last, axis=0))
        out[peer] = jnp.concatenate([grads, packed], axis=0).astype(BF16)


def first_sum(recv, slots, share):
    kept = slots - fold(slots, share)[2]

    def body(*refs):
        first_sum_kernel(slots, *refs)

    return pl.pallas_call(
        body,
        in_specs=[vmem()],
        out_specs=vmem(),
        out_shape=jax.ShapeDtypeStruct((SIDE, kept + PAD // 2, LANES), BF16),
        compiler_params=params(32),
        name="first_sum",
    )(recv)


def second_sum_kernel(slots, share, recv, out):
    rows = out.shape[0]
    experts = rows // PAD
    spare, parts, rest = fold(slots, share)
    kept = slots - rest
    sums = total(recv, 0, recv.shape[1])
    side = iota((rest, LANES), 1)
    last = jnp.zeros((rest, LANES), F32)
    for q in range(parts):
        piece = pltpu.roll(sums[q * rest : (q + 1) * rest], (q + 1) * spare, axis=1)
        last = jnp.where((side >= q * spare) & (side < (q + 1) * spare), piece, last)
    grads = jnp.concatenate([sums[:kept], last], axis=0)
    probs = unpack_sums(sums[kept:])
    probs = jnp.concatenate([probs, pltpu.roll(probs, LANES - LANES // 4, axis=1)], axis=0)
    line = dot(one_hot(iota((slots, PAD), 0) // experts == iota((slots, PAD), 1)), probs.astype(BF16))
    lane, row = iota((slots, LANES), 1), iota((slots, LANES), 0)
    column = jnp.sum(jnp.where(lane == row % experts, line, 0.0), axis=1, keepdims=True)
    values = jnp.where(lane < share, grads, jnp.where(lane == share, column, 0.0)).astype(BF16)
    out[...] = swap(jnp.concatenate([values, jnp.zeros((rows - slots, LANES), BF16)], axis=0))


def second_sum(recv, slots, share, experts):
    def body(*refs):
        second_sum_kernel(slots, share, *refs)

    return pl.pallas_call(
        body,
        in_specs=[vmem()],
        out_specs=vmem(),
        out_shape=jax.ShapeDtypeStruct((experts * PAD, LANES), BF16),
        compiler_params=params(32),
        name="second_sum",
    )(recv)


def combine_kernel(routes, picker, recv, in_grad, prob_grad):
    share = in_grad.shape[1]
    hot = picker[...]
    values = swap(recv[...])[: hot.shape[0]]
    summed = lax.dot_general(hot, values, (((0,), (0,)), ((), ())), preferred_element_type=F32)
    in_grad[...] = summed[:, :share].astype(BF16)
    column = values[:, share : share + 1].astype(F32)
    found = jnp.where(hot.astype(F32) > 0.0, column, 0.0)
    expert = iota(hot.shape, 0) % PAD
    for k in range(routes.shape[0]):
        hit = routes[k : k + 1, :] == expert
        prob_grad[k : k + 1, :] = jnp.sum(jnp.where(hit, found, 0.0), axis=0, keepdims=True)


def combine(routes, picker, recv, share):
    choices, tokens = routes.shape
    return pl.pallas_call(
        combine_kernel,
        in_specs=[vmem()] * 3,
        out_specs=[vmem()] * 2,
        out_shape=[
            jax.ShapeDtypeStruct((tokens, share), BF16),
            jax.ShapeDtypeStruct((choices, tokens), F32),
        ],
        compiler_params=params(32),
        name="combine",
    )(routes, picker, recv)


def exchange(values):
    return lax.all_to_all(values, "expert", split_axis=0, concat_axis=0, tiled=True)


def exchange_in_plane(values, even_along_x):
    experts = lax.axis_size("expert")
    groups = []
    for expert in range(experts):
        along_x = (expert % 2 == 0) == even_along_x
        for line in range(SIDE):
            group = [(line, i) if along_x else (i, line) for i in range(SIDE)]
            groups.append([(y * SIDE + x) * experts + expert for y, x in group])
    return lax.all_to_all(
        values, ("y", "x", "expert"), split_axis=0, concat_axis=0, axis_index_groups=groups, tiled=True
    )


def on_device(routes, probs, out_grad, saved_inputs, w_gate, w_up, w_down):
    experts = lax.axis_size("expert")
    capacity = saved_inputs.shape[2]
    width = out_grad.shape[1]
    share = width // (SIDE * SIDE)
    slots = experts * capacity
    routes = routes.T
    probs = probs.T
    at_x, at_y, expert = (
        lax.axis_index(axis).astype(jnp.int32).reshape(1) for axis in ("x", "y", "expert")
    )

    send, picker = pick(at_x, at_y, expert, routes, probs, out_grad, capacity, experts)
    recv = exchange(send.reshape(experts, -1, LANES)).reshape(-1, LANES)
    inputs = saved_inputs[0].transpose(1, 0, 2).reshape(slots, width)
    factors = forward(inputs, w_gate[0], w_up[0])
    down = w_down[0].T

    shards, scale = spread(recv, factors, down, width // SIDE, capacity)
    grads = exchange_in_plane(shards, True)
    parts = slot_grads(
        expert, grads, down, factors, scale, w_gate[0], w_up[0], capacity
    )
    first = first_sum(exchange_in_plane(parts, False), slots, share)
    back = second_sum(exchange_in_plane(first, True), slots, share, experts)
    got = exchange(back.reshape(experts, PAD, LANES)).reshape(experts * PAD, LANES)
    in_grad, prob_grad = combine(routes, picker, got, share)
    return in_grad, prob_grad.T


def solution(mesh):
    grid = Mesh(mesh.devices.reshape(SIDE, SIDE, -1), ("y", "x", "expert"))
    dp = ("y", "x")
    placed = (
        P("expert", None),
        P("expert", None),
        P("expert", None),
        P("expert", None, None, None),
        P("expert", dp, None),
        P("expert", dp, None),
        P("expert", dp, None),
    )
    return jax.shard_map(
        on_device,
        mesh=grid,
        in_specs=placed,
        out_specs=(P("expert", dp), P("expert", None)),
        check_vma=False,
    )
```

```python
import jax
import jax.numpy as jnp
from jax import lax
from jax.experimental import pallas as pl
from jax.experimental.pallas import tpu as pltpu
from jax.sharding import Mesh
from jax.sharding import PartitionSpec as P

F32 = jnp.float32
BF16 = jnp.bfloat16
LANES = 128
PAD = 16
SIDE = 8
MIB = 1024 * 1024
HELD = jnp.bfloat16


def iota(shape, dim):
    return lax.broadcasted_iota(jnp.int32, shape, dim)


def one_hot(mask):
    return jnp.where(mask, 1.0, 0.0).astype(BF16)


def dot(a, b):
    return jnp.dot(a, b, preferred_element_type=F32)


def swap(values):
    row, source = iota((PAD * PAD, PAD * PAD), 0), iota((PAD * PAD, PAD * PAD), 1)
    order = one_hot(source == (row % PAD) * PAD + row // PAD)
    return dot(order, values).astype(values.dtype)


def params(mib):
    return pltpu.CompilerParams(vmem_limit_bytes=mib * MIB)


def vmem():
    return pl.BlockSpec(memory_space=pltpu.VMEM)


def hbm():
    return pl.BlockSpec(memory_space=pltpu.HBM)


def smem():
    return pl.BlockSpec(memory_space=pltpu.SMEM)


def pick_kernel(
    capacity, at_x, at_y, _, routes_in, probs_in, out_grad, send, picker, routes, probs, grad_x, grad_y, sems
):
    slots, tokens = picker.shape
    experts = slots // capacity
    tiles = grad_x.shape[1] // LANES
    copies = [
        pltpu.make_async_copy(routes_in, routes, sems.at[0]),
        pltpu.make_async_copy(probs_in, probs, sems.at[1]),
    ]
    for axis, (at, grad) in enumerate(((at_x, grad_x), (at_y, grad_y))):
        width = grad.shape[1]
        first = pl.multiple_of(at[0] * width, LANES)
        copies.append(
            pltpu.make_async_copy(out_grad.at[:, pl.ds(first, width)], grad, sems.at[2 + axis])
        )
    for copy in copies:
        copy.start()
    copies[0].wait()
    copies[1].wait()
    row = iota((slots, tokens), 0)
    expert, slot = row % experts, row // experts
    named = jnp.zeros((slots, tokens), F32)
    weight = jnp.zeros((slots, tokens), F32)
    rounded = probs[...].astype(BF16).astype(F32)
    for k in range(routes.shape[0]):
        hit = routes[k : k + 1, :] == expert
        named = named + jnp.where(hit, 1.0, 0.0)
        weight = weight + jnp.where(hit, rounded[k : k + 1, :], 0.0)
    earlier = one_hot(iota((tokens, tokens), 0) < iota((tokens, tokens), 1))
    before = dot(named.astype(BF16), earlier)
    chosen = (named > 0.0) & (before == slot.astype(F32))
    hot = one_hot(chosen)
    picker[...] = hot
    scale = jnp.sum(jnp.where(chosen, weight, 0.0), axis=1, keepdims=True)
    lane = iota((experts, LANES), 1)
    weights = jnp.zeros((experts, LANES), F32)
    for c in range(capacity):
        weights = jnp.where(lane == c, scale[c * experts : (c + 1) * experts], weights)
    copies[2].wait()
    copies[3].wait()
    even = iota((slots, LANES), 0) % 2 == 0
    pieces = []
    for j in range(tiles):
        columns = slice(j * LANES, (j + 1) * LANES)
        picked = jnp.where(even, dot(hot, grad_y[:, columns]), dot(hot, grad_x[:, columns]))
        pieces.append(picked.astype(BF16))
    chunk = send.shape[0] // experts
    spare = chunk - tiles * capacity - 1
    pieces += [weights.astype(BF16), jnp.zeros((spare * experts, LANES), BF16)]
    rows = jnp.concatenate(pieces, axis=0)
    for g in range(chunk // PAD):
        group = swap(rows[g * PAD * PAD : (g + 1) * PAD * PAD])
        for e in range(experts):
            send[e * chunk + g * PAD : e * chunk + (g + 1) * PAD, :] = group[e * PAD : (e + 1) * PAD]


def pick(at_x, at_y, expert, routes, probs, out_grad, capacity, experts):
    tokens, width = out_grad.shape
    part = width // SIDE
    choices = routes.shape[0]
    chunk = -(-(part // LANES * capacity + 1) // PAD) * PAD

    def body(*refs):
        pick_kernel(capacity, *refs)

    return pl.pallas_call(
        body,
        in_specs=[smem(), smem(), smem(), hbm(), hbm(), hbm()],
        out_specs=[vmem()] * 2,
        out_shape=[
            jax.ShapeDtypeStruct((experts * chunk, LANES), BF16),
            jax.ShapeDtypeStruct((experts * capacity, tokens), BF16),
        ],
        scratch_shapes=[
            pltpu.VMEM((choices, tokens), jnp.int32),
            pltpu.VMEM((choices, tokens), F32),
            pltpu.VMEM((tokens, part), BF16),
            pltpu.VMEM((tokens, part), BF16),
            pltpu.SemaphoreType.DMA((4,)),
        ],
        compiler_params=params(63),
        name="pick",
    )(at_x, at_y, expert, routes, probs, out_grad)


def spread_kernel(capacity, recv, factors, down, out, scale):
    chunk = recv.shape[0] // PAD
    moved = []
    for g in range(chunk // PAD):
        group = [recv[s * chunk + g * PAD : s * chunk + (g + 1) * PAD, :] for s in range(PAD)]
        moved.append(swap(jnp.concatenate(group, axis=0)))
    rows = jnp.concatenate(moved, axis=0)
    kept = out.shape[1]
    for peer in range(out.shape[0]):
        out[peer] = rows[:kept]
    weights = rows[kept : kept + PAD].astype(F32)
    for c in range(capacity):
        column = jnp.broadcast_to(weights[:, c : c + 1], (PAD, LANES))
        scale[c * PAD : (c + 1) * PAD, :] = column


def spread(recv, factors, down, part, capacity):
    slots = PAD * capacity
    kept = part // LANES * slots

    def body(*refs):
        spread_kernel(capacity, *refs)

    return pl.pallas_call(
        body,
        in_specs=[vmem()] + [pl.BlockSpec(memory_space=pl.ANY)] * 2,
        out_specs=[vmem(), vmem()],
        out_shape=[
            jax.ShapeDtypeStruct((SIDE, kept, LANES), BF16),
            jax.ShapeDtypeStruct((slots, LANES), F32),
        ],
        compiler_params=params(32),
        name="spread",
    )(recv, factors, down)


def forward_kernel(inputs, gate_in, up_in, factors, gate_pre, up_pre):
    contract = (((1,), (1,)), ((), ()))
    step = pl.program_id(0)
    x = inputs[...]
    gate_part = lax.dot_general(x, gate_in[...], contract, preferred_element_type=F32)
    up_part = lax.dot_general(x, up_in[...], contract, preferred_element_type=F32)

    @pl.when(step == 0)
    def _():
        gate_pre[...] = gate_part
        up_pre[...] = up_part

    @pl.when(step > 0)
    def _():
        gate_pre[...] += gate_part
        up_pre[...] += up_part

    @pl.when(step == pl.num_programs(0) - 1)
    def _():
        gate, up = gate_pre[...], up_pre[...]
        sigmoid_gate = jax.nn.sigmoid(gate)
        silu_gate = gate * sigmoid_gate
        factors[0] = (silu_gate * up).astype(BF16).astype(F32)
        factors[1] = up * sigmoid_gate * (1.0 + gate * (1.0 - sigmoid_gate))
        factors[2] = silu_gate


def forward(inputs, w_gate, w_up):
    slots, width = inputs.shape
    hidden = w_gate.shape[0]
    steps = 4
    piece = lambda rows: pl.BlockSpec((rows, width // steps), lambda i: (0, i))
    return pl.pallas_call(
        forward_kernel,
        grid=(steps,),
        in_specs=[piece(slots), piece(hidden), piece(hidden)],
        out_specs=pl.BlockSpec((3, slots, hidden), lambda i: (0, 0, 0)),
        out_shape=jax.ShapeDtypeStruct((3, slots, hidden), F32),
        scratch_shapes=[pltpu.VMEM((slots, hidden), F32)] * 2,
        compiler_params=params(32),
        cost_estimate=pl.CostEstimate(
            flops=4 * slots * hidden * width,
            bytes_accessed=4 * width * (slots + 2 * hidden),
            transcendentals=0,
        ),
        name="forward",
    )(inputs, w_gate, w_up)


def pack_sums(total):
    high = total.astype(BF16).astype(F32)
    return jnp.where(iota(total.shape, 1) < LANES // 2, high, total - high).astype(BF16)


def unpack_sums(packed):
    return packed + pltpu.roll(packed, LANES // 2, axis=1)


def cut(source, first, width, lane):
    done = 0
    while done < width:
        src, dst = first + done, lane + done
        take = min(width - done, LANES - src % LANES, LANES - dst % LANES)
        shift = (dst - src) % LANES
        values = source(src // LANES)
        if shift:
            values = pltpu.roll(values, shift, axis=1)
        yield dst // LANES, dst % LANES, dst % LANES + take, values
        done += take


def slot_grads_kernel(
    capacity, expert, grads, down, factors, scale, w_gate, w_up, out, held
):
    peers, slots = grads.shape[0], scale.shape[0]
    part = down.shape[0] // peers
    tiles = [
        grads[peer, j * slots : (j + 1) * slots, :]
        for peer in range(peers)
        for j in range(part // LANES)
    ]
    back = dot(jnp.concatenate(tiles, axis=1), down[...])
    sums = jnp.sum(factors[0] * back, axis=1, keepdims=True)
    scaled = scale[:, :1] * back
    d_gate, d_up = (scaled * factors[1]).astype(BF16), (scaled * factors[2]).astype(BF16)

    d_both = jnp.concatenate([d_gate, d_up], axis=1)
    experts = slots // capacity
    grid = jnp.where(iota((slots, LANES), 1) % (LANES // 2) == iota((slots, LANES), 0) % experts, sums, 0.0)
    rows = [jnp.sum(grid[c * experts : (c + 1) * experts], axis=0, keepdims=True) for c in range(capacity)]
    total = jnp.zeros((PAD, LANES), F32)
    for c, line in enumerate(rows):
        total = jnp.where(iota((PAD, LANES), 0) == c, line, total)
    packed = pack_sums(total)

    block = w_gate.shape[1] // SIDE
    tiles = block // LANES
    share = block // SIDE
    for y in range(SIDE):
        columns = slice(y * block, (y + 1) * block)
        grad = dot(d_both, jnp.concatenate([w_gate[:, columns], w_up[:, columns]], axis=0))
        held[:, columns] = grad.astype(held.dtype)
    for peer in range(SIDE):
        out[peer, tiles * slots :, :] = packed

    def tile_of(tile):
        return held[:, tile * LANES : (tile + 1) * LANES]

    @pl.when(expert[0] % 2 == 1)
    def _():
        lane = iota((slots, LANES), 1)
        for x in range(SIDE):
            made = [None] * tiles
            for y in range(SIDE):
                for tile, low, high, values in cut(tile_of, y * block + x * share, share, y * share):
                    if made[tile] is None:
                        made[tile] = values
                    else:
                        made[tile] = jnp.where((lane >= low) & (lane < high), values, made[tile])
            for j in range(tiles):
                out[x, j * slots : (j + 1) * slots, :] = made[j].astype(BF16)

    @pl.when(expert[0] % 2 == 0)
    def _():
        for y in range(SIDE):
            for j in range(tiles):
                out[y, j * slots : (j + 1) * slots, :] = tile_of(y * tiles + j).astype(BF16)


def slot_grads(expert, grads, down, factors, scale, w_gate, w_up, capacity):
    slots = scale.shape[0]
    width = w_gate.shape[1]
    rows = width // SIDE // LANES * slots + PAD

    def body(*refs):
        slot_grads_kernel(capacity, *refs)

    return pl.pallas_call(
        body,
        in_specs=[smem()] + [vmem()] * 6,
        out_specs=vmem(),
        out_shape=jax.ShapeDtypeStruct((SIDE, rows, LANES), BF16),
        scratch_shapes=[pltpu.VMEM((slots, width), HELD)],
        compiler_params=params(32),
        name="slot_grads",
    )(expert, grads, down, factors, scale, w_gate, w_up)


def total(recv, first, count):
    sums = recv[0, first : first + count].astype(F32)
    for peer in range(1, recv.shape[0]):
        sums = sums + recv[peer, first : first + count].astype(F32)
    return sums


def fold(slots, share):
    spare = LANES - share
    parts = share // spare
    rest = slots // (parts + 1)
    return spare, parts, rest


def first_sum_kernel(slots, recv, out):
    peers, rows, _ = recv.shape
    tiles = (rows - PAD) // slots
    share = tiles * LANES // peers
    spare, parts, rest = fold(slots, share)
    kept = slots - rest
    columns = [total(recv, j * slots, slots) for j in range(tiles)]
    sums = unpack_sums(total(recv, tiles * slots, PAD))
    half = PAD // 2
    packed = pack_sums(sums[:half] + pltpu.roll(sums[half:], LANES // 4, axis=1)).astype(F32)
    lane = iota((slots, LANES), 1)
    for peer in range(peers):
        made = None
        for _, low, high, values in cut(lambda tile: columns[tile], peer * share, share, 0):
            made = values if made is None else jnp.where((lane >= low) & (lane < high), values, made)
        last = [pltpu.roll(made[kept:], share - q * spare, axis=1) for q in range(parts)]
        grads = jnp.where(lane[:kept] < share, made[:kept], jnp.concatenate(last, axis=0))
        out[peer] = jnp.concatenate([grads, packed], axis=0).astype(BF16)


def first_sum(recv, slots, share):
    kept = slots - fold(slots, share)[2]

    def body(*refs):
        first_sum_kernel(slots, *refs)

    return pl.pallas_call(
        body,
        in_specs=[vmem()],
        out_specs=vmem(),
        out_shape=jax.ShapeDtypeStruct((SIDE, kept + PAD // 2, LANES), BF16),
        compiler_params=params(32),
        name="first_sum",
    )(recv)


def second_sum_kernel(slots, share, recv, out):
    rows = out.shape[0]
    experts = rows // PAD
    spare, parts, rest = fold(slots, share)
    kept = slots - rest
    sums = total(recv, 0, recv.shape[1])
    side = iota((rest, LANES), 1)
    last = jnp.zeros((rest, LANES), F32)
    for q in range(parts):
        piece = pltpu.roll(sums[q * rest : (q + 1) * rest], (q + 1) * spare, axis=1)
        last = jnp.where((side >= q * spare) & (side < (q + 1) * spare), piece, last)
    grads = jnp.concatenate([sums[:kept], last], axis=0)
    probs = unpack_sums(sums[kept:])
    probs = jnp.concatenate([probs, pltpu.roll(probs, LANES - LANES // 4, axis=1)], axis=0)
    line = dot(one_hot(iota((slots, PAD), 0) // experts == iota((slots, PAD), 1)), probs.astype(BF16))
    lane, row = iota((slots, LANES), 1), iota((slots, LANES), 0)
    column = jnp.sum(jnp.where(lane == row % experts, line, 0.0), axis=1, keepdims=True)
    values = jnp.where(lane < share, grads, jnp.where(lane == share, column, 0.0)).astype(BF16)
    out[...] = swap(jnp.concatenate([values, jnp.zeros((rows - slots, LANES), BF16)], axis=0))


def second_sum(recv, slots, share, experts):
    def body(*refs):
        second_sum_kernel(slots, share, *refs)

    return pl.pallas_call(
        body,
        in_specs=[vmem()],
        out_specs=vmem(),
        out_shape=jax.ShapeDtypeStruct((experts * PAD, LANES), BF16),
        compiler_params=params(32),
        name="second_sum",
    )(recv)


def combine_kernel(routes, picker, recv, in_grad, prob_grad):
    share = in_grad.shape[1]
    hot = picker[...]
    values = swap(recv[...])[: hot.shape[0]]
    summed = lax.dot_general(hot, values, (((0,), (0,)), ((), ())), preferred_element_type=F32)
    in_grad[...] = summed[:, :share].astype(BF16)
    column = values[:, share : share + 1].astype(F32)
    found = jnp.where(hot.astype(F32) > 0.0, column, 0.0)
    expert = iota(hot.shape, 0) % PAD
    for k in range(routes.shape[0]):
        hit = routes[k : k + 1, :] == expert
        prob_grad[k : k + 1, :] = jnp.sum(jnp.where(hit, found, 0.0), axis=0, keepdims=True)


def combine(routes, picker, recv, share):
    choices, tokens = routes.shape
    return pl.pallas_call(
        combine_kernel,
        in_specs=[vmem()] * 3,
        out_specs=[vmem()] * 2,
        out_shape=[
            jax.ShapeDtypeStruct((tokens, share), BF16),
            jax.ShapeDtypeStruct((choices, tokens), F32),
        ],
        compiler_params=params(32),
        name="combine",
    )(routes, picker, recv)


def exchange(values):
    return lax.all_to_all(values, "expert", split_axis=0, concat_axis=0, tiled=True)


def exchange_in_plane(values, even_along_x):
    experts = lax.axis_size("expert")
    groups = []
    for expert in range(experts):
        along_x = (expert % 2 == 0) == even_along_x
        for line in range(SIDE):
            group = [(line, i) if along_x else (i, line) for i in range(SIDE)]
            groups.append([(y * SIDE + x) * experts + expert for y, x in group])
    return lax.all_to_all(
        values, ("y", "x", "expert"), split_axis=0, concat_axis=0, axis_index_groups=groups, tiled=True
    )


def on_device(routes, probs, out_grad, saved_inputs, w_gate, w_up, w_down):
    experts = lax.axis_size("expert")
    capacity = saved_inputs.shape[2]
    width = out_grad.shape[1]
    share = width // (SIDE * SIDE)
    slots = experts * capacity
    routes = routes.T
    probs = probs.T
    at_x, at_y, expert = (
        lax.axis_index(axis).astype(jnp.int32).reshape(1) for axis in ("x", "y", "expert")
    )

    send, picker = pick(at_x, at_y, expert, routes, probs, out_grad, capacity, experts)
    recv = exchange(send.reshape(experts, -1, LANES)).reshape(-1, LANES)
    inputs = saved_inputs[0].transpose(1, 0, 2).reshape(slots, width)
    factors = forward(inputs, w_gate[0], w_up[0])
    down = w_down[0].T

    shards, scale = spread(recv, factors, down, width // SIDE, capacity)
    grads = exchange_in_plane(shards, False)
    parts = slot_grads(
        expert, grads, down, factors, scale, w_gate[0], w_up[0], capacity
    )
    first = first_sum(exchange_in_plane(parts, False), slots, share)
    back = second_sum(exchange_in_plane(first, True), slots, share, experts)
    got = exchange(back.reshape(experts, PAD, LANES)).reshape(experts * PAD, LANES)
    in_grad, prob_grad = combine(routes, picker, got, share)
    return in_grad, prob_grad.T


def solution(mesh):
    grid = Mesh(mesh.devices.reshape(SIDE, SIDE, -1), ("y", "x", "expert"))
    dp = ("y", "x")
    placed = (
        P("expert", None),
        P("expert", None),
        P("expert", None),
        P("expert", None, None, None),
        P("expert", dp, None),
        P("expert", dp, None),
        P("expert", dp, None),
    )
    return jax.shard_map(
        on_device,
        mesh=grid,
        in_specs=placed,
        out_specs=(P("expert", dp), P("expert", None)),
        check_vma=False,
    )
```
